32 devices in a mesh: rows: 8 (over y, x, core), cols: 4 (over z).
Axes of the slice: x: 2, y: 2, z: 4, core: 2. Of those that a mesh axis runs over, the one named last changes fastest.
Arguments:
- known_inverse: bfloat16 [4, 8, 32, 1024], P(None, 'rows', None, 'cols'), may hold values from -6 to 6
- lower_panel: bfloat16 [4, 4, 8, 32, 512], P(None, 'cols'), may hold values from -0.1875 to 0.1875
- chain_panel: bfloat16 [4, 512, 512], replicated, may hold values from -0.25 to 0.25
- diag_inverse: float32 [4, 512, 512], P(None, 'rows'), may hold values from -6 to 6
- top_cols: bfloat16 [4, 8, 32, 512], P('cols', 'rows'), may hold values from -6 to 6
- top_diag: float32 [512, 512], P('rows'), may hold values from -6 to 6
- pattern: int32 [4, 32], replicated, may hold values from 0 to 1, as said below
Outputs:
- inverse_cols: bfloat16 [4, 4, 8, 32, 512], P(None, 'cols', 'rows')
- inverse_diag: float32 [4, 512, 512], P(None, 'rows')
- inverse_sub: float32 [4, 512, 512], P(None, 'rows')
The draws below stay inside these ranges and needn't reach their ends.
Inputs may be any that keep to these rules, and one draw needn't show every extreme that they name: `pattern`: row k marks exactly (32 * (5 + k)) // 9 block rows, and every block row marked in row k is marked in row k + 1.
All inputs are finite; a program needn't handle non-finite values.
Results may differ from the reference program's by a relative error of at most 0.025.
Values may be sent and summed in bfloat16 or wider, within the bound.
No kernel may reach another device: no remote copies, remote signals or barrier semaphores. Data moves between devices by JAX's collectives and lax.ppermute only.
A program may use at most 128 MiB of HBM per device.

```python
import jax
import jax.numpy as jnp
from jax import lax

W = 512
PIECE = 32
SUPERS = 4
NU = 1024
N_ROWS = 8
N_COLS = 4


def draw_pattern(key, part):
    total = N_COLS * N_ROWS
    ranking = jax.random.permutation(key, total)
    section = jnp.arange(SUPERS, dtype=jnp.int32)
    marked = total * (SUPERS + 1 + section) // (2 * SUPERS + 1)
    return (ranking[None, :] < marked[:, None]).astype(jnp.int32)


def levels(rng, shape, shards, low, high):
    loudness, own = 1.0, jax.random.fold_in(rng, 6)
    for axis_at, shards_of in shards:
        heights = jnp.exp(jax.random.uniform(jax.random.fold_in(own, axis_at), (shards_of,), jnp.float32, low / len(shards), high / len(shards)))
        loudness = loudness * jnp.repeat(heights, shape[axis_at] // shards_of).reshape([-1 if axis == axis_at else 1 for axis in range(len(shape))])
    return loudness


def noise(stream_key, dims, deviation, reach, split=(), kind=jnp.bfloat16):
    factor_of = levels(stream_key, dims, split, -0.22, 0.18) if split else 1.0
    drawn = jax.random.normal(stream_key, dims, jnp.float32) * deviation * factor_of
    return jnp.minimum(jnp.maximum(drawn, -reach), reach).astype(kind)


def setup_inputs(seed: int = 0) -> dict:
    key_list = jax.random.split(jax.random.key(seed), 8)
    known_inverse = noise(key_list[0], (N_COLS, N_ROWS, PIECE, NU), 1.0, 6.0, ((1, 8), (3, 4)))
    lower_panel = noise(key_list[1], (SUPERS, N_COLS, N_ROWS, PIECE, W), NU ** -0.5, 0.1875, ((1, 4),))
    chain_panel = noise(key_list[2], (SUPERS, W, W), W ** -0.5, 0.25)
    diag_inverse = noise(key_list[3], (SUPERS, W, W), 1.0, 6.0, ((1, 8),), jnp.float32)
    top_cols = noise(key_list[4], (N_COLS, N_ROWS, PIECE, W), 1.0, 6.0, ((0, 4), (1, 8)))
    top_diag = noise(key_list[5], (W, W), 1.0, 6.0, ((0, 8),), jnp.float32)
    pattern = draw_pattern(jax.random.fold_in(key_list[7], 71), 0)
    return dict(known_inverse=known_inverse, lower_panel=lower_panel, chain_panel=chain_panel, diag_inverse=diag_inverse, top_cols=top_cols, top_diag=top_diag, pattern=pattern)


def reference(known_inverse, lower_panel, chain_panel, diag_inverse, top_cols, top_diag, pattern):
    order = N_COLS * N_ROWS * PIECE
    ancestor = known_inverse.reshape(order, order)
    block_mask = pattern.astype(jnp.bfloat16)
    masked_panel = (lower_panel.reshape(SUPERS, N_COLS * N_ROWS, PIECE, W) * block_mask[:, :, None, None]).reshape(SUPERS, order, W)
    stacked = jnp.transpose(masked_panel, (1, 0, 2)).reshape(order, SUPERS * W)
    col_span = order // N_COLS
    running = jnp.zeros((order, SUPERS * W), jnp.float32)
    for column in range(N_COLS):
        part_cols = ancestor[:, column * col_span:(column + 1) * col_span]
        part_rows = stacked[column * col_span:(column + 1) * col_span]
        rounded = jnp.dot(part_cols, part_rows, preferred_element_type=jnp.float32).astype(jnp.bfloat16)
        rounded = lax.optimization_barrier(rounded)
        running = running + rounded.astype(jnp.float32)
    product_all = running.reshape(order, SUPERS, W)
    prev_cols = top_cols.reshape(order, W)
    prev_diag = top_diag
    cols_list = [None] * SUPERS
    diag_list = [None] * SUPERS
    sub_list = [None] * SUPERS
    for section in reversed(range(SUPERS)):
        link_block = chain_panel[section]
        link_wide = link_block.astype(jnp.float32)
        row_mask = jnp.repeat(pattern[section].astype(jnp.float32), PIECE)
        carried = jnp.dot(prev_cols, link_block, preferred_element_type=jnp.float32)
        new_cols = (-(product_all[:, section] + carried) * row_mask[:, None]).astype(jnp.bfloat16)
        sub_block = -(jnp.dot(prev_cols.T, masked_panel[section], preferred_element_type=jnp.float32)
                      + jnp.dot(prev_diag, link_wide, precision=lax.Precision.HIGHEST))
        diag_block = (diag_inverse[section]
                      - jnp.dot(masked_panel[section].T, new_cols, preferred_element_type=jnp.float32)
                      - jnp.dot(link_wide.T, sub_block, precision=lax.Precision.HIGHEST))
        cols_list[section] = new_cols.reshape(N_COLS, N_ROWS, PIECE, W)
        diag_list[section] = diag_block
        sub_list[section] = sub_block
        prev_cols = new_cols
        prev_diag = diag_block
    return jnp.stack(cols_list), jnp.stack(diag_list), jnp.stack(sub_list)
```

```python
import jax
import jax.numpy as jnp
from jax import lax
from jax.sharding import PartitionSpec as P

BF = jnp.bfloat16
F32 = jnp.float32


def dot(a, b):
    return jnp.dot(a, b, preferred_element_type=F32)


def dot_nt(a, b):
    return lax.dot_general(a, b, (((1,), (1,)), ((), ())), preferred_element_type=F32)


def pow2(n):
    return n & (n - 1) == 0


def target(i, j, n):
    return i ^ j if pow2(n) else (i + j) % n


def source(i, j, n):
    return i ^ j if pow2(n) else (i - j) % n


def hop(x, axis, j):
    n = lax.axis_size(axis)
    return lax.ppermute(x, axis, [(i, target(i, j, n)) for i in range(n)])


def gather_rows(x):
    n = lax.axis_size("rows")
    me = lax.axis_index("rows")
    if n == 8:
        parts = [x] + [hop(x, "rows", j) for j in (6, 4, 2)]
        offsets = [0, 6, 4, 2]
        here = jnp.stack(parts)
        there = hop(here, "rows", 1)
        whole = jnp.concatenate([here, there], 0)
        offsets = offsets + [o ^ 1 for o in offsets]
        return whole, [source(me, o, n) for o in offsets]
    if pow2(n):
        whole, offsets, bit = x[None], [0], n // 2
        while bit:
            whole = jnp.concatenate([whole, hop(whole, "rows", bit)], 0)
            offsets = offsets + [o ^ bit for o in offsets]
            bit //= 2
        return whole, [source(me, o, n) for o in offsets]
    return lax.all_gather(x, "rows"), list(range(n))


def scatter_cols(pieces):
    n = lax.axis_size("cols")
    me = lax.axis_index("cols")
    total = lax.dynamic_index_in_dim(pieces, me, 0, False).astype(F32)
    for j in reversed(range(1, n)):
        sent = lax.dynamic_index_in_dim(pieces, target(me, j, n), 0, False)
        total = total + hop(sent, "cols", j).astype(F32)
    return total


def gather_cols(x):
    n = lax.axis_size("cols")
    me = lax.axis_index("cols")
    whole = jnp.zeros((n,) + x.shape, x.dtype)
    got = [(me, x)] + [(source(me, j, n), hop(x, "cols", j)) for j in reversed(range(1, n))]
    for at, piece in got:
        whole = lax.dynamic_update_index_in_dim(whole, piece, at, 0)
    return whole


def local(known_inverse, lower_panel, chain_panel, diag_inverse, top_cols, top_diag, pattern):
    n_rows = lax.axis_size("rows")
    n_cols = lax.axis_size("cols")
    row_id = lax.axis_index("rows")
    col_id = lax.axis_index("cols")
    supers = lower_panel.shape[0]
    piece = known_inverse.shape[2]
    width = lower_panel.shape[-1]
    share = width // n_rows
    known = known_inverse.reshape(n_cols * piece, -1)
    group_mask = lax.dynamic_slice_in_dim(pattern, col_id * n_rows, n_rows, 1).astype(BF)
    panels = lower_panel[:, 0] * group_mask[:, :, None, None]
    own_mask = lax.dynamic_index_in_dim(group_mask, row_id, 1, keepdims=False).astype(F32)

    slabs = panels.reshape(supers, n_rows * piece, width)
    partial = jnp.stack([dot(known, slabs[k]).astype(BF).reshape(n_cols, piece, width) for k in range(supers)], 1)
    product = scatter_cols(partial)

    start = [top_diag] + [diag_inverse[k] for k in reversed(range(1, supers))]
    level_of = lambda c: supers - c
    mine = jnp.zeros((share, width), F32)
    for i, s in enumerate(start):
        mine = jnp.where(col_id % len(start) == i, s, mine) if n_cols <= len(start) else jnp.where(col_id == i, s, mine)
    joined = jnp.concatenate([mine.astype(BF), top_cols.reshape(piece, width)], 0)
    gathered, order = gather_rows(joined)
    shares = gathered[:, :share].reshape(width, width)
    tops = gathered[:, share:].reshape(n_rows * piece, width)
    order = jnp.stack([jnp.asarray(o, jnp.int32) for o in order])
    panel_rel = [p[order].reshape(n_rows * piece, width) for p in panels]
    own_rows = (lax.broadcasted_iota(jnp.int32, (share, width), 1) == row_id * share + lax.broadcasted_iota(jnp.int32, (share, width), 0)).astype(BF)
    stacks = [own_rows]
    for k in range(supers):
        stacks.append(jnp.concatenate([dot_nt(stacks[k], chain_panel[k]).astype(BF), own_rows], 0))
    begins = []
    for k in range(supers + 1):
        rel = stacks[k].reshape(-1, n_rows, share)[:, order].reshape(-1, width)
        begins.append(dot(rel, shares))
    reach = [dot_nt(stacks[k], panel_rel[k]).astype(BF) for k in range(supers)]

    prev = top_cols.reshape(piece, width)
    cols_list = [None] * supers
    for k in reversed(range(supers)):
        carried = dot(prev, chain_panel[k])
        prev = (-(product[k] + carried) * own_mask[k]).astype(BF)
        cols_list[k] = prev
    cols_out = jnp.stack(cols_list)
    all_cols, _ = gather_rows(cols_out)
    slab_cols = [all_cols[:, k].reshape(n_rows * piece, width) for k in range(supers)] + [tops]

    acc = jnp.where(col_id == 0, begins[supers], 0.0)
    diag_list = [None] * supers
    sub_list = [None] * supers
    for k in reversed(range(supers)):
        across = dot_nt(stacks[k + 1], slab_cols[k + 1]).astype(BF)
        full = dot(acc.astype(BF), chain_panel[k]) + dot(across, panel_rel[k])
        sub_list[k] = -full[(k + 1) * share:]
        acc = full[: (k + 1) * share] - dot(reach[k], slab_cols[k])
        diag_list[k] = acc[k * share :]
        if k:
            acc = acc + jnp.where(col_id == level_of(k), begins[k], 0.0)
    done = jnp.stack(diag_list + sub_list)
    if share % n_cols == 0:
        part = share // n_cols
        pieces = jnp.swapaxes(done.astype(BF).reshape(2 * supers, n_cols, part, width), 0, 1)
        summed = gather_cols(scatter_cols(pieces).astype(BF))
        summed = jnp.swapaxes(summed, 0, 1).reshape(2 * supers, share, width)
    else:
        summed = lax.psum(done.astype(BF), "cols")
    summed = summed.astype(F32)
    return (
        cols_out.reshape(supers, 1, 1, piece, width),
        diag_inverse + summed[:supers],
        summed[supers:],
    )


def solution(mesh):
    in_specs = (
        P(None, "rows", None, "cols"),
        P(None, "cols", None, None, None),
        P(),
        P(None, "rows", None),
        P("cols", "rows", None, None),
        P("rows", None),
        P(),
    )
    out_specs = (P(None, "cols", "rows", None, None), P(None, "rows", None), P(None, "rows", None))
    return jax.shard_map(local, mesh=mesh, in_specs=in_specs, out_specs=out_specs, check_vma=False)
```

```python
import functools

import jax
import jax.numpy as jnp
from jax import lax
from jax.experimental import pallas as pl
from jax.experimental.pallas import tpu as pltpu
from jax.sharding import PartitionSpec as P

BF = jnp.bfloat16
F32 = jnp.float32
ROW_ORDER = (0, 6, 4, 2, 1, 7, 5, 3)
VMEM_BYTES = 32 << 20


def dot(a, b):
    return jnp.dot(a, b, preferred_element_type=F32)


def dot_nt(a, b):
    return lax.dot_general(a, b, (((1,), (1,)), ((), ())), preferred_element_type=F32)


def pow2(n):
    return n & (n - 1) == 0


def target(i, j, n):
    return i ^ j if pow2(n) else (i + j) % n


def source(i, j, n):
    return i ^ j if pow2(n) else (i - j) % n


def hop(x, axis, j):
    n = lax.axis_size(axis)
    return lax.ppermute(x, axis, [(i, target(i, j, n)) for i in range(n)])


def gather_rows(x):
    n = lax.axis_size("rows")
    me = lax.axis_index("rows")
    if n == 8:
        parts = [x] + [hop(x, "rows", j) for j in (6, 4, 2)]
        offsets = [0, 6, 4, 2]
        here = jnp.stack(parts)
        there = hop(here, "rows", 1)
        whole = jnp.concatenate([here, there], 0)
        offsets = offsets + [o ^ 1 for o in offsets]
        return whole, [source(me, o, n) for o in offsets]
    if pow2(n):
        whole, offsets, bit = x[None], [0], n // 2
        while bit:
            whole = jnp.concatenate([whole, hop(whole, "rows", bit)], 0)
            offsets = offsets + [o ^ bit for o in offsets]
            bit //= 2
        return whole, [source(me, o, n) for o in offsets]
    return lax.all_gather(x, "rows"), list(range(n))


def scatter_cols(pieces):
    n = lax.axis_size("cols")
    me = lax.axis_index("cols")
    total = lax.dynamic_index_in_dim(pieces, me, 0, False).astype(F32)
    for j in reversed(range(1, n)):
        sent = lax.dynamic_index_in_dim(pieces, target(me, j, n), 0, False)
        total = total + hop(sent, "cols", j).astype(F32)
    return total


def gather_cols(x):
    n = lax.axis_size("cols")
    me = lax.axis_index("cols")
    whole = jnp.zeros((n,) + x.shape, x.dtype)
    got = [(me, x)] + [(source(me, j, n), hop(x, "cols", j)) for j in reversed(range(1, n))]
    for at, piece in got:
        whole = lax.dynamic_update_index_in_dim(whole, piece, at, 0)
    return whole


def general(known_inverse, lower_panel, chain_panel, diag_inverse, top_cols, top_diag, pattern):
    n_rows = lax.axis_size("rows")
    n_cols = lax.axis_size("cols")
    row_id = lax.axis_index("rows")
    col_id = lax.axis_index("cols")
    supers = lower_panel.shape[0]
    piece = known_inverse.shape[2]
    width = lower_panel.shape[-1]
    share = width // n_rows
    known = known_inverse.reshape(n_cols * piece, -1)
    group_mask = lax.dynamic_slice_in_dim(pattern, col_id * n_rows, n_rows, 1).astype(BF)
    panels = lower_panel[:, 0] * group_mask[:, :, None, None]
    own_mask = lax.dynamic_index_in_dim(group_mask, row_id, 1, keepdims=False).astype(F32)

    slabs = panels.reshape(supers, n_rows * piece, width)
    partial = jnp.stack([dot(known, slabs[k]).astype(BF).reshape(n_cols, piece, width) for k in range(supers)], 1)
    product = scatter_cols(partial)

    start = [top_diag] + [diag_inverse[k] for k in reversed(range(1, supers))]
    level_of = lambda c: supers - c
    mine = jnp.zeros((share, width), F32)
    for i, s in enumerate(start):
        mine = jnp.where(col_id % len(start) == i, s, mine) if n_cols <= len(start) else jnp.where(col_id == i, s, mine)
    joined = jnp.concatenate([mine.astype(BF), top_cols.reshape(piece, width)], 0)
    gathered, order = gather_rows(joined)
    shares = gathered[:, :share].reshape(width, width)
    tops = gathered[:, share:].reshape(n_rows * piece, width)
    order = jnp.stack([jnp.asarray(o, jnp.int32) for o in order])
    panel_rel = [p[order].reshape(n_rows * piece, width) for p in panels]
    own_rows = (lax.broadcasted_iota(jnp.int32, (share, width), 1) == row_id * share + lax.broadcasted_iota(jnp.int32, (share, width), 0)).astype(BF)
    stacks = [own_rows]
    for k in range(supers):
        stacks.append(jnp.concatenate([dot_nt(stacks[k], chain_panel[k]).astype(BF), own_rows], 0))
    begins = []
    for k in range(supers + 1):
        rel = stacks[k].reshape(-1, n_rows, share)[:, order].reshape(-1, width)
        begins.append(dot(rel, shares))
    reach = [dot_nt(stacks[k], panel_rel[k]).astype(BF) for k in range(supers)]

    prev = top_cols.reshape(piece, width)
    cols_list = [None] * supers
    for k in reversed(range(supers)):
        carried = dot(prev, chain_panel[k])
        prev = (-(product[k] + carried) * own_mask[k]).astype(BF)
        cols_list[k] = prev
    cols_out = jnp.stack(cols_list)
    all_cols, _ = gather_rows(cols_out)
    slab_cols = [all_cols[:, k].reshape(n_rows * piece, width) for k in range(supers)] + [tops]

    acc = jnp.where(col_id == 0, begins[supers], 0.0)
    diag_list = [None] * supers
    sub_list = [None] * supers
    for k in reversed(range(supers)):
        across = dot_nt(stacks[k + 1], slab_cols[k + 1]).astype(BF)
        full = dot(acc.astype(BF), chain_panel[k]) + dot(across, panel_rel[k])
        sub_list[k] = -full[(k + 1) * share:]
        acc = full[: (k + 1) * share] - dot(reach[k], slab_cols[k])
        diag_list[k] = acc[k * share :]
        if k:
            acc = acc + jnp.where(col_id == level_of(k), begins[k], 0.0)
    done = jnp.stack(diag_list + sub_list)
    if share % n_cols == 0:
        part = share // n_cols
        pieces = jnp.swapaxes(done.astype(BF).reshape(2 * supers, n_cols, part, width), 0, 1)
        summed = gather_cols(scatter_cols(pieces).astype(BF))
        summed = jnp.swapaxes(summed, 0, 1).reshape(2 * supers, share, width)
    else:
        summed = lax.psum(done.astype(BF), "cols")
    summed = summed.astype(F32)
    return (
        cols_out.reshape(supers, 1, 1, piece, width),
        diag_inverse + summed[:supers],
        summed[supers:],
    )


def first_kernel(n_cols, n_rows, g_ref, m_ref, pattern_ref, diag_ref, top_ref, tops_ref, panel_ref, joined_ref, *piece_refs):
    col = lax.axis_index("cols")
    supers, _, piece, width = m_ref.shape
    share = top_ref.shape[0]
    for k in range(supers):
        for r in range(n_rows):
            on = pattern_ref[k, col * n_rows + r].astype(F32)
            panel_ref[k, pl.ds(r * piece, piece)] = (m_ref[k, r].astype(F32) * on).astype(BF)
    for j, out in enumerate(piece_refs):
        rows = g_ref[col ^ j]
        for k in range(supers):
            out[k] = dot(rows, panel_ref[k]).astype(BF)
    mine = jnp.zeros((share, width), F32)
    for i in range(supers):
        begin = top_ref[...] if i == 0 else diag_ref[supers - i]
        mine = jnp.where(col == i, begin, mine)
    joined_ref[pl.ds(0, share)] = mine.astype(BF)
    joined_ref[pl.ds(share, piece)] = tops_ref[...]


def chain_kernel(n_cols, n_rows, l_ref, tops_ref, pattern_ref, own_ref, *refs):
    *got_refs, cols_ref = refs
    supers = own_ref.shape[0]
    at = lax.axis_index("cols") * n_rows + lax.axis_index("rows")
    prev = tops_ref[...]
    for k in reversed(range(supers)):
        total = own_ref[k].astype(F32)
        for got in got_refs:
            total = total + got[k].astype(F32)
        total = total + dot(prev, l_ref[k])
        prev = (-(total * pattern_ref[k, at].astype(F32))).astype(BF)
        cols_ref[k] = prev


def place(refs, order, write):
    me = lax.axis_index("rows")
    for ref, offset in zip(refs, order):
        write(me ^ offset, ref)


def ready_kernel(n_cols, n_rows, order, l_ref, panel_ref, *refs):
    got = refs[: len(order)]
    stacks_ref, reach_ref, begin_ref, ahead_ref, x_ref, y_ref, all_ref = refs[len(order) :]
    supers, width, _ = l_ref.shape
    share = width // n_rows
    piece = y_ref.shape[0] // n_rows
    col, row = lax.axis_index("cols"), lax.axis_index("rows")

    def write(at, ref):
        x_ref[pl.ds(pl.multiple_of(at * share, share), share)] = ref[pl.ds(0, share)]
        y_ref[pl.ds(pl.multiple_of(at * piece, piece), piece)] = ref[pl.ds(share, piece)]

    place(got, order, write)
    lane = lax.broadcasted_iota(jnp.int32, (share, width), 1)
    sub = lax.broadcasted_iota(jnp.int32, (share, width), 0)
    unit = jnp.where(lane == row * share + sub, 1.0, 0.0).astype(BF)
    stack = unit
    all_ref[...] = jnp.zeros_like(all_ref)
    all_ref[0, pl.ds(0, share)] = unit
    at = 0
    for k in range(supers):
        reach_ref[pl.ds(at, (k + 1) * share)] = dot_nt(stack, panel_ref[k]).astype(BF)
        at += (k + 1) * share
        stack = jnp.concatenate([dot_nt(stack, l_ref[k]).astype(BF), unit], 0)
        all_ref[k + 1, pl.ds(0, (k + 2) * share)] = stack
    at = 0
    for k in range(1, supers):
        stacks_ref[pl.ds(at, (k + 1) * share)] = all_ref[k, pl.ds(0, (k + 1) * share)]
        at += (k + 1) * share
    begin = dot(all_ref[jnp.maximum(supers - col, 0)], x_ref[...])
    begin_ref[...] = begin
    first = jnp.where(col == 0, begin, 0.0).astype(BF)
    across = dot_nt(stack, y_ref[...]).astype(BF)
    ahead_ref[...] = dot(first, l_ref[supers - 1]) + dot(across, panel_ref[supers - 1])


def rows_kernel(n_cols, n_rows, order, l_ref, panel_ref, stacks_ref, reach_ref, begin_ref, ahead_ref, *refs):
    got = refs[: len(order)]
    pieces = refs[len(order) : len(order) + n_cols]
    y_ref, done_ref = refs[len(order) + n_cols :]
    supers, width, _ = l_ref.shape
    share = width // n_rows
    piece = y_ref.shape[1] // n_rows
    part = share // n_cols
    col = lax.axis_index("cols")

    def write(at, ref):
        for k in range(supers):
            y_ref[k, pl.ds(pl.multiple_of(at * piece, piece), piece)] = ref[k]

    place(got, order, write)
    full = ahead_ref[...]
    stack_at = sum((k + 1) * share for k in range(1, supers))
    reach_at = sum((k + 1) * share for k in range(supers))
    for k in reversed(range(supers)):
        here = (k + 1) * share
        if k < supers - 1:
            stack_at -= here + share
            across = dot_nt(stacks_ref[pl.ds(stack_at, here + share)], y_ref[k + 1]).astype(BF)
            full = dot(acc.astype(BF), l_ref[k]) + dot(across, panel_ref[k])
        reach_at -= here
        acc = full[:here] - dot(reach_ref[pl.ds(reach_at, here)], y_ref[k])
        done_ref[supers + k] = -full[here:]
        done_ref[k] = acc[k * share :]
        if k:
            acc = acc + jnp.where(col == supers - k, begin_ref[pl.ds(0, here)], 0.0)
    for j, out in enumerate(pieces):
        at = pl.multiple_of((col ^ j) * part, part)
        for i in range(2 * supers):
            out[i] = done_ref[i, pl.ds(at, part)].astype(BF)


def sum_kernel(own_ref, *refs):
    *got_refs, out_ref = refs
    for i in range(own_ref.shape[0]):
        total = own_ref[i].astype(F32)
        for got in got_refs:
            total = total + got[i].astype(F32)
        out_ref[i] = total.astype(BF)


def last_kernel(n_cols, diag_ref, *refs):
    *got_refs, diag_out, sub_out = refs
    supers = diag_ref.shape[0]
    part = got_refs[0].shape[1]
    col = lax.axis_index("cols")
    for j, got in enumerate(got_refs):
        rows = pl.ds(pl.multiple_of((col ^ j) * part, part), part)
        for k in range(supers):
            diag_out[k, rows] = diag_ref[k, rows] + got[k].astype(F32)
            sub_out[k, rows] = got[supers + k].astype(F32)


def call(kernel, outs, *args, scratch=(), smem=(), flops=0, moved=0):
    vmem = pl.BlockSpec(memory_space=pltpu.VMEM)
    return pl.pallas_call(
        kernel,
        out_shape=tuple(jax.ShapeDtypeStruct(s, d) for s, d in outs),
        in_specs=[pl.BlockSpec(memory_space=pltpu.SMEM) if i in smem else vmem for i in range(len(args))],
        out_specs=tuple(vmem for _ in outs),
        scratch_shapes=[pltpu.VMEM(s, d) for s, d in scratch],
        compiler_params=pltpu.CompilerParams(vmem_limit_bytes=VMEM_BYTES),
        cost_estimate=pl.CostEstimate(flops=flops, bytes_accessed=moved, transcendentals=0),
    )(*args)


def exchange_rows(x):
    near = [x] + [hop(x, "rows", j) for j in ROW_ORDER[1:4]]
    return near + [hop(p, "rows", 1) for p in near]


def local(known_inverse, lower_panel, chain_panel, diag_inverse, top_cols, top_diag, pattern):
    n_rows = lax.axis_size("rows")
    n_cols = lax.axis_size("cols")
    supers = lower_panel.shape[0]
    piece = known_inverse.shape[2]
    width = lower_panel.shape[-1]
    share = width // n_rows
    if n_rows != len(ROW_ORDER) or not pow2(n_cols) or n_cols < supers or share % (16 * n_cols) or piece % 16:
        return general(known_inverse, lower_panel, chain_panel, diag_inverse, top_cols, top_diag, pattern)
    known = known_inverse[:, 0]
    tops = top_cols[0, 0]
    block = n_rows * piece
    ways = range(1, n_cols)
    rows_of = [(k + 1) * share for k in range(supers + 1)]
    panel, joined, own, *sent = call(
        functools.partial(first_kernel, n_cols, n_rows),
        [((supers, block, width), BF), ((share + piece, width), BF)] + [((supers, piece, width), BF)] * n_cols,
        known, lower_panel[:, 0], pattern, diag_inverse, top_diag, tops, smem=(2,),
        flops=2 * known.size * supers * width, moved=4 * block * width * supers,
    )
    got = [hop(sent[j - 1], "cols", j) for j in reversed(ways)]
    around = exchange_rows(joined)
    stacks, reach, begin, ahead = call(
        functools.partial(ready_kernel, n_cols, n_rows, ROW_ORDER),
        [((sum(rows_of[1:supers]), width), BF), ((sum(rows_of[:supers]), block), BF), ((rows_of[supers], width), F32), ((rows_of[supers], width), F32)],
        chain_panel, panel, *around,
        scratch=[((width, width), BF), ((block, width), BF), ((supers + 1, rows_of[supers], width), BF)],
        flops=2 * 8 * share * width * width * 4, moved=4 * width * width * supers,
    )
    (cols,) = call(
        functools.partial(chain_kernel, n_cols, n_rows),
        [((supers, piece, width), BF)],
        chain_panel, tops, pattern, own, *got, smem=(2,),
        flops=2 * piece * width * width * supers, moved=2 * width * width * supers,
    )
    pieces = call(
        functools.partial(rows_kernel, n_cols, n_rows, ROW_ORDER),
        [((2 * supers, share // n_cols, width), BF)] * n_cols,
        chain_panel, panel, stacks, reach, begin, ahead, *exchange_rows(cols),
        scratch=[((supers, block, width), BF), ((2 * supers, share, width), F32)],
        flops=2 * 20 * share * width * width, moved=4 * width * width * supers,
    )
    got = [hop(pieces[j], "cols", j) for j in reversed(ways)]
    (summed,) = call(sum_kernel, [(pieces[0].shape, BF)], pieces[0], *got)
    there = {j: hop(summed, "cols", j) for j in reversed(ways)}
    diag, sub = call(
        functools.partial(last_kernel, n_cols),
        [(diag_inverse.shape, F32)] * 2,
        diag_inverse, summed, *[there[j] for j in ways],
    )
    return cols.reshape(supers, 1, 1, piece, width), diag, sub


def solution(mesh):
    in_specs = (
        P(None, "rows", None, "cols"),
        P(None, "cols", None, None, None),
        P(),
        P(None, "rows", None),
        P("cols", "rows", None, None),
        P("rows", None),
        P(),
    )
    out_specs = (P(None, "cols", "rows", None, None), P(None, "rows", None), P(None, "rows", None))
    return jax.shard_map(local, mesh=mesh, in_specs=in_specs, out_specs=out_specs, check_vma=False)
```

```python
import functools

import jax
import jax.numpy as jnp
from jax import lax
from jax.experimental import pallas as pl
from jax.experimental.pallas import tpu as pltpu
from jax.sharding import PartitionSpec as P

BF = jnp.bfloat16
F32 = jnp.float32
ROW_ORDER = (0, 6, 4, 2, 1, 7, 5, 3)
VMEM_BYTES = 32 << 20


def dot(a, b):
    return jnp.dot(a, b, preferred_element_type=F32)


def dot_nt(a, b):
    return lax.dot_general(a, b, (((1,), (1,)), ((), ())), preferred_element_type=F32)


def pow2(n):
    return n & (n - 1) == 0


def target(i, j, n):
    return i ^ j if pow2(n) else (i + j) % n


def source(i, j, n):
    return i ^ j if pow2(n) else (i - j) % n


def hop(x, axis, j):
    n = lax.axis_size(axis)
    return lax.ppermute(x, axis, [(i, target(i, j, n)) for i in range(n)])


def gather_rows(x):
    n = lax.axis_size("rows")
    me = lax.axis_index("rows")
    if n == 8:
        parts = [x] + [hop(x, "rows", j) for j in (6, 4, 2)]
        offsets = [0, 6, 4, 2]
        here = jnp.stack(parts)
        there = hop(here, "rows", 1)
        whole = jnp.concatenate([here, there], 0)
        offsets = offsets + [o ^ 1 for o in offsets]
        return whole, [source(me, o, n) for o in offsets]
    if pow2(n):
        whole, offsets, bit = x[None], [0], n // 2
        while bit:
            whole = jnp.concatenate([whole, hop(whole, "rows", bit)], 0)
            offsets = offsets + [o ^ bit for o in offsets]
            bit //= 2
        return whole, [source(me, o, n) for o in offsets]
    return lax.all_gather(x, "rows"), list(range(n))


def scatter_cols(pieces):
    n = lax.axis_size("cols")
    me = lax.axis_index("cols")
    total = lax.dynamic_index_in_dim(pieces, me, 0, False).astype(F32)
    for j in reversed(range(1, n)):
        sent = lax.dynamic_index_in_dim(pieces, target(me, j, n), 0, False)
        total = total + hop(sent, "cols", j).astype(F32)
    return total


def gather_cols(x):
    n = lax.axis_size("cols")
    me = lax.axis_index("cols")
    whole = jnp.zeros((n,) + x.shape, x.dtype)
    got = [(me, x)] + [(source(me, j, n), hop(x, "cols", j)) for j in reversed(range(1, n))]
    for at, piece in got:
        whole = lax.dynamic_update_index_in_dim(whole, piece, at, 0)
    return whole


def general(known_inverse, lower_panel, chain_panel, diag_inverse, top_cols, top_diag, pattern):
    n_rows = lax.axis_size("rows")
    n_cols = lax.axis_size("cols")
    row_id = lax.axis_index("rows")
    col_id = lax.axis_index("cols")
    supers = lower_panel.shape[0]
    piece = known_inverse.shape[2]
    width = lower_panel.shape[-1]
    share = width // n_rows
    known = known_inverse.reshape(n_cols * piece, -1)
    group_mask = lax.dynamic_slice_in_dim(pattern, col_id * n_rows, n_rows, 1).astype(BF)
    panels = lower_panel[:, 0] * group_mask[:, :, None, None]
    own_mask = lax.dynamic_index_in_dim(group_mask, row_id, 1, keepdims=False).astype(F32)

    slabs = panels.reshape(supers, n_rows * piece, width)
    partial = jnp.stack([dot(known, slabs[k]).astype(BF).reshape(n_cols, piece, width) for k in range(supers)], 1)
    product = scatter_cols(partial)

    start = [top_diag] + [diag_inverse[k] for k in reversed(range(1, supers))]
    level_of = lambda c: supers - c
    mine = jnp.zeros((share, width), F32)
    for i, s in enumerate(start):
        mine = jnp.where(col_id % len(start) == i, s, mine) if n_cols <= len(start) else jnp.where(col_id == i, s, mine)
    joined = jnp.concatenate([mine.astype(BF), top_cols.reshape(piece, width)], 0)
    gathered, order = gather_rows(joined)
    shares = gathered[:, :share].reshape(width, width)
    tops = gathered[:, share:].reshape(n_rows * piece, width)
    order = jnp.stack([jnp.asarray(o, jnp.int32) for o in order])
    panel_rel = [p[order].reshape(n_rows * piece, width) for p in panels]
    own_rows = (lax.broadcasted_iota(jnp.int32, (share, width), 1) == row_id * share + lax.broadcasted_iota(jnp.int32, (share, width), 0)).astype(BF)
    stacks = [own_rows]
    for k in range(supers):
        stacks.append(jnp.concatenate([dot_nt(stacks[k], chain_panel[k]).astype(BF), own_rows], 0))
    begins = []
    for k in range(supers + 1):
        rel = stacks[k].reshape(-1, n_rows, share)[:, order].reshape(-1, width)
        begins.append(dot(rel, shares))
    reach = [dot_nt(stacks[k], panel_rel[k]).astype(BF) for k in range(supers)]

    prev = top_cols.reshape(piece, width)
    cols_list = [None] * supers
    for k in reversed(range(supers)):
        carried = dot(prev, chain_panel[k])
        prev = (-(product[k] + carried) * own_mask[k]).astype(BF)
        cols_list[k] = prev
    cols_out = jnp.stack(cols_list)
    all_cols, _ = gather_rows(cols_out)
    slab_cols = [all_cols[:, k].reshape(n_rows * piece, width) for k in range(supers)] + [tops]

    acc = jnp.where(col_id == 0, begins[supers], 0.0)
    diag_list = [None] * supers
    sub_list = [None] * supers
    for k in reversed(range(supers)):
        across = dot_nt(stacks[k + 1], slab_cols[k + 1]).astype(BF)
        full = dot(acc.astype(BF), chain_panel[k]) + dot(across, panel_rel[k])
        sub_list[k] = -full[(k + 1) * share:]
        acc = full[: (k + 1) * share] - dot(reach[k], slab_cols[k])
        diag_list[k] = acc[k * share :]
        if k:
            acc = acc + jnp.where(col_id == level_of(k), begins[k], 0.0)
    done = jnp.stack(diag_list + sub_list)
    if share % n_cols == 0:
        part = share // n_cols
        pieces = jnp.swapaxes(done.astype(BF).reshape(2 * supers, n_cols, part, width), 0, 1)
        summed = gather_cols(scatter_cols(pieces).astype(BF))
        summed = jnp.swapaxes(summed, 0, 1).reshape(2 * supers, share, width)
    else:
        summed = lax.psum(done.astype(BF), "cols")
    summed = summed.astype(F32)
    return (
        cols_out.reshape(supers, 1, 1, piece, width),
        diag_inverse + summed[:supers],
        summed[supers:],
    )


def fetch(source, into, sem):
    copy = pltpu.make_async_copy(source, into, sem)
    copy.start()
    return copy


def first_kernel(n_cols, n_rows, g_any, m_any, pattern_any, *refs):
    panel_ref, mask_ref = refs[:2]
    piece_refs = refs[2 : 2 + n_cols]
    g_ref, m_ref, pattern_ref, sems = refs[2 + n_cols :]
    col, row = lax.axis_index("cols"), lax.axis_index("rows")
    supers, _, piece, _ = m_ref.shape
    pattern_copy = fetch(pattern_any, pattern_ref, sems.at[0])
    panel_copies = [fetch(m_any.at[k], m_ref.at[k], sems.at[1 + k]) for k in range(supers)]
    g_copy = fetch(g_any, g_ref, sems.at[1 + supers])
    pattern_copy.wait()
    for k in range(supers):
        mask_ref[k] = jnp.full(mask_ref.shape[1:], pattern_ref[k, col * n_rows + row].astype(F32))
        panel_copies[k].wait()
        if k == 0:
            g_copy.wait()
        for r in range(n_rows):
            on = pattern_ref[k, col * n_rows + r].astype(F32)
            panel_ref[k, pl.ds(r * piece, piece)] = (m_ref[k, r].astype(F32) * on).astype(BF)
        for j, out in enumerate(piece_refs):
            out[k] = dot(g_ref[col ^ j], panel_ref[k]).astype(BF)


def chain_kernel(l_ref, joined_ref, mask_ref, own_ref, *refs):
    *got_refs, cols_ref, copy_ref = refs
    supers, piece, _ = own_ref.shape
    prev = joined_ref[pl.ds(joined_ref.shape[0] - piece, piece)]
    for k in reversed(range(supers)):
        total = own_ref[k].astype(F32)
        for got in got_refs:
            total = total + got[k].astype(F32)
        total = total + dot(prev, l_ref[k])
        prev = (-(total * mask_ref[k, pl.ds(0, 1)])).astype(BF)
        cols_ref[k] = prev
        copy_ref[k] = prev


def place(refs, order, write):
    me = lax.axis_index("rows")
    for ref, offset in zip(refs, order):
        write(me ^ offset, ref)


def ready_kernel(n_cols, n_rows, l_any, diag_any, top_any, tops_any, panel_ref, *refs):
    l_ref, stacks_ref, reach_ref, joined_ref, begin_ref, tops_ref, sems = refs
    supers, width, _ = l_ref.shape
    share, piece = width // n_rows, tops_ref.shape[0]
    col, row = lax.axis_index("cols"), lax.axis_index("rows")
    copies = [fetch(l_any.at[k], l_ref.at[k], sems.at[k]) for k in range(supers)]
    tops_copy = fetch(tops_any, tops_ref, sems.at[supers])

    @pl.when(col == 0)
    def _():
        fetch(top_any, begin_ref, sems.at[supers + 1]).wait()

    @pl.when(jnp.logical_and(col > 0, col < supers))
    def _():
        fetch(diag_any.at[jnp.clip(supers - col, 1, supers - 1)], begin_ref, sems.at[supers + 1]).wait()

    @pl.when(col >= supers)
    def _():
        begin_ref[...] = jnp.zeros_like(begin_ref)

    tops_copy.wait()
    joined_ref[pl.ds(0, share)] = begin_ref[...].astype(BF)
    joined_ref[pl.ds(share, piece)] = tops_ref[...]
    lane = lax.broadcasted_iota(jnp.int32, (share, width), 1)
    sub = lax.broadcasted_iota(jnp.int32, (share, width), 0)
    unit = jnp.where(lane == row * share + sub, 1.0, 0.0).astype(BF)
    stacks_ref[...] = jnp.zeros_like(stacks_ref)
    stacks_ref[0, pl.ds(0, share)] = unit
    stack, at = unit, 0
    for k in range(supers):
        reach_ref[pl.ds(at, (k + 1) * share)] = dot_nt(stack, panel_ref[k]).astype(BF)
        at += (k + 1) * share
        copies[k].wait()
        stack = jnp.concatenate([dot_nt(stack, l_ref[k]).astype(BF), unit], 0)
        stacks_ref[k + 1, pl.ds(0, (k + 2) * share)] = stack


def place(refs, order, write):
    me = lax.axis_index("rows")
    for ref, offset in zip(refs, order):
        write(me ^ offset, ref)


def begin_kernel(n_cols, n_rows, order, l_ref, panel_ref, stacks_ref, *refs):
    got = refs[: len(order)]
    begin_ref, ahead_ref, x_ref, y_ref = refs[len(order) :]
    supers, width, _ = l_ref.shape
    share, piece = width // n_rows, y_ref.shape[0] // n_rows
    col = lax.axis_index("cols")

    def write(at, ref):
        x_ref[pl.ds(pl.multiple_of(at * share, share), share)] = ref[pl.ds(0, share)]
        y_ref[pl.ds(pl.multiple_of(at * piece, piece), piece)] = ref[pl.ds(share, piece)]

    place(got, order, write)
    begin = dot(stacks_ref[jnp.maximum(supers - col, 0)], x_ref[...])
    begin_ref[...] = begin
    first = jnp.where(col == 0, begin, 0.0).astype(BF)
    across = dot_nt(stacks_ref[supers], y_ref[...]).astype(BF)
    ahead_ref[...] = dot(first, l_ref[supers - 1]) + dot(across, panel_ref[supers - 1])


def rows_kernel(n_cols, n_rows, order, l_ref, panel_ref, stacks_ref, reach_ref, begin_ref, ahead_ref, *refs):
    got = refs[: len(order)]
    pieces = refs[len(order) : len(order) + n_cols]
    y_ref, done_ref = refs[len(order) + n_cols :]
    supers, width, _ = l_ref.shape
    share = width // n_rows
    piece = y_ref.shape[1] // n_rows
    part = share // n_cols
    col = lax.axis_index("cols")

    def write(at, ref):
        for k in range(supers):
            y_ref[k, pl.ds(pl.multiple_of(at * piece, piece), piece)] = ref[k]

    place(got, order, write)
    full = ahead_ref[...]
    reach_at = sum((k + 1) * share for k in range(supers))
    for k in reversed(range(supers)):
        here = (k + 1) * share
        if k < supers - 1:
            across = dot_nt(stacks_ref[k + 1, pl.ds(0, here + share)], y_ref[k + 1]).astype(BF)
            full = dot(acc.astype(BF), l_ref[k]) + dot(across, panel_ref[k])
        reach_at -= here
        acc = full[:here] - dot(reach_ref[pl.ds(reach_at, here)], y_ref[k])
        done_ref[supers + k] = -full[here:]
        done_ref[k] = acc[k * share :]
        if k:
            acc = acc + jnp.where(col == supers - k, begin_ref[pl.ds(0, here)], 0.0)
    for j, out in enumerate(pieces):
        at = pl.multiple_of((col ^ j) * part, part)
        for i in range(2 * supers):
            out[i] = done_ref[i, pl.ds(at, part)].astype(BF)


def sum_kernel(own_ref, *refs):
    *got_refs, out_ref = refs
    for i in range(own_ref.shape[0]):
        total = own_ref[i].astype(F32)
        for got in got_refs:
            total = total + got[i].astype(F32)
        out_ref[i] = total.astype(BF)


def last_kernel(n_cols, diag_ref, *refs):
    *got_refs, diag_out, sub_out = refs
    supers = diag_ref.shape[0]
    part = got_refs[0].shape[1]
    col = lax.axis_index("cols")
    for j, got in enumerate(got_refs):
        rows = pl.ds(pl.multiple_of((col ^ j) * part, part), part)
        for k in range(supers):
            diag_out[k, rows] = diag_ref[k, rows] + got[k].astype(F32)
            sub_out[k, rows] = got[supers + k].astype(F32)


def call(kernel, outs, *args, scratch=(), away=(), flops=0, moved=0):
    vmem, hbm = pl.BlockSpec(memory_space=pltpu.VMEM), pl.BlockSpec(memory_space=pltpu.HBM)
    return pl.pallas_call(
        kernel,
        out_shape=tuple(jax.ShapeDtypeStruct(s, d) for s, d in outs),
        in_specs=[hbm if i in away else vmem for i in range(len(args))],
        out_specs=tuple(vmem for _ in outs),
        scratch_shapes=scratch,
        compiler_params=pltpu.CompilerParams(vmem_limit_bytes=VMEM_BYTES),
        cost_estimate=pl.CostEstimate(flops=flops, bytes_accessed=moved, transcendentals=0),
    )(*args)


def exchange_rows(x):
    near = [x] + [hop(x, "rows", j) for j in ROW_ORDER[1:4]]
    return near + [hop(p, "rows", 1) for p in near]


def local(known_inverse, lower_panel, chain_panel, diag_inverse, top_cols, top_diag, pattern):
    n_rows = lax.axis_size("rows")
    n_cols = lax.axis_size("cols")
    supers = lower_panel.shape[0]
    piece = known_inverse.shape[2]
    width = lower_panel.shape[-1]
    share = width // n_rows
    if n_rows != len(ROW_ORDER) or not pow2(n_cols) or n_cols < supers or share % (16 * n_cols) or piece % 16:
        return general(known_inverse, lower_panel, chain_panel, diag_inverse, top_cols, top_diag, pattern)
    known = known_inverse[:, 0]
    tops = top_cols[0, 0]
    block = n_rows * piece
    ways = range(1, n_cols)
    rows_of = [(k + 1) * share for k in range(supers + 1)]
    panel, mask, own, *sent = call(
        functools.partial(first_kernel, n_cols, n_rows),
        [((supers, block, width), BF), ((supers, 8, width), F32)] + [((supers, piece, width), BF)] * n_cols,
        known, lower_panel[:, 0], pattern, away=range(3),
        scratch=[
            pltpu.VMEM(known.shape, BF), pltpu.VMEM((supers, n_rows, piece, width), BF),
            pltpu.SMEM(pattern.shape, jnp.int32), pltpu.SemaphoreType.DMA((2 + supers,)),
        ],
        flops=2 * known.size * supers * width, moved=4 * block * width * supers,
    )
    got = [hop(sent[j - 1], "cols", j) for j in reversed(ways)]
    links, stacks, reach, joined = call(
        functools.partial(ready_kernel, n_cols, n_rows),
        [(chain_panel.shape, BF), ((supers + 1, rows_of[supers], width), BF), ((sum(rows_of[:supers]), block), BF), ((share + piece, width), BF)],
        chain_panel, diag_inverse, top_diag, tops, panel, away=range(4),
        scratch=[pltpu.VMEM((share, width), F32), pltpu.VMEM((piece, width), BF), pltpu.SemaphoreType.DMA((supers + 2,))],
        flops=2 * 12 * share * width * width, moved=4 * width * width * supers,
    )
    begin, ahead = call(
        functools.partial(begin_kernel, n_cols, n_rows, ROW_ORDER),
        [((rows_of[supers], width), F32)] * 2,
        links, panel, stacks, *exchange_rows(joined),
        scratch=[pltpu.VMEM((width, width), BF), pltpu.VMEM((block, width), BF)],
        flops=2 * 15 * share * width * width, moved=4 * width * width,
    )
    cols, cols_out = call(
        chain_kernel,
        [((supers, piece, width), BF)] * 2,
        links, joined, mask, own, *got,
        flops=2 * piece * width * width * supers, moved=2 * width * width * supers,
    )
    pieces = call(
        functools.partial(rows_kernel, n_cols, n_rows, ROW_ORDER),
        [((2 * supers, share // n_cols, width), BF)] * n_cols,
        links, panel, stacks, reach, begin, ahead, *exchange_rows(cols),
        scratch=[pltpu.VMEM((supers, block, width), BF), pltpu.VMEM((2 * supers, share, width), F32)],
        flops=2 * 20 * share * width * width, moved=4 * width * width * supers,
    )
    got = [hop(pieces[j], "cols", j) for j in reversed(ways)]
    (summed,) = call(sum_kernel, [(pieces[0].shape, BF)], pieces[0], *got)
    there = {j: hop(summed, "cols", j) for j in reversed(ways)}
    diag, sub = call(
        functools.partial(last_kernel, n_cols),
        [(diag_inverse.shape, F32)] * 2,
        diag_inverse, summed, *[there[j] for j in ways],
    )
    return cols_out.reshape(supers, 1, 1, piece, width), diag, sub


def solution(mesh):
    in_specs = (
        P(None, "rows", None, "cols"),
        P(None, "cols", None, None, None),
        P(),
        P(None, "rows", None),
        P("cols", "rows", None, None),
        P("rows", None),
        P(),
    )
    out_specs = (P(None, "cols", "rows", None, None), P(None, "rows", None), P(None, "rows", None))
    return jax.shard_map(local, mesh=mesh, in_specs=in_specs, out_specs=out_specs, check_vma=False)
```

```python
import functools

import jax
import jax.numpy as jnp
from jax import lax
from jax.experimental import pallas as pl
from jax.experimental.pallas import tpu as pltpu
from jax.sharding import PartitionSpec as P

BF = jnp.bfloat16
F32 = jnp.float32
ROW_ORDER = (0, 6, 4, 2, 1, 7, 5, 3)
VMEM_BYTES = 32 << 20


def dot(a, b):
    return jnp.dot(a, b, preferred_element_type=F32)


def dot_nt(a, b):
    return lax.dot_general(a, b, (((1,), (1,)), ((), ())), preferred_element_type=F32)


def pow2(n):
    return n & (n - 1) == 0


def target(i, j, n):
    return i ^ j if pow2(n) else (i + j) % n


def source(i, j, n):
    return i ^ j if pow2(n) else (i - j) % n


def hop(x, axis, j):
    n = lax.axis_size(axis)
    return lax.ppermute(x, axis, [(i, target(i, j, n)) for i in range(n)])


def gather_rows(x):
    n = lax.axis_size("rows")
    me = lax.axis_index("rows")
    if n == 8:
        parts = [x] + [hop(x, "rows", j) for j in (6, 4, 2)]
        offsets = [0, 6, 4, 2]
        here = jnp.stack(parts)
        there = hop(here, "rows", 1)
        whole = jnp.concatenate([here, there], 0)
        offsets = offsets + [o ^ 1 for o in offsets]
        return whole, [source(me, o, n) for o in offsets]
    if pow2(n):
        whole, offsets, bit = x[None], [0], n // 2
        while bit:
            whole = jnp.concatenate([whole, hop(whole, "rows", bit)], 0)
            offsets = offsets + [o ^ bit for o in offsets]
            bit //= 2
        return whole, [source(me, o, n) for o in offsets]
    return lax.all_gather(x, "rows"), list(range(n))


def scatter_cols(pieces):
    n = lax.axis_size("cols")
    me = lax.axis_index("cols")
    total = lax.dynamic_index_in_dim(pieces, me, 0, False).astype(F32)
    for j in reversed(range(1, n)):
        sent = lax.dynamic_index_in_dim(pieces, target(me, j, n), 0, False)
        total = total + hop(sent, "cols", j).astype(F32)
    return total


def gather_cols(x):
    n = lax.axis_size("cols")
    me = lax.axis_index("cols")
    whole = jnp.zeros((n,) + x.shape, x.dtype)
    got = [(me, x)] + [(source(me, j, n), hop(x, "cols", j)) for j in reversed(range(1, n))]
    for at, piece in got:
        whole = lax.dynamic_update_index_in_dim(whole, piece, at, 0)
    return whole


def general(known_inverse, lower_panel, chain_panel, diag_inverse, top_cols, top_diag, pattern):
    n_rows = lax.axis_size("rows")
    n_cols = lax.axis_size("cols")
    row_id = lax.axis_index("rows")
    col_id = lax.axis_index("cols")
    supers = lower_panel.shape[0]
    piece = known_inverse.shape[2]
    width = lower_panel.shape[-1]
    share = width // n_rows
    known = known_inverse.reshape(n_cols * piece, -1)
    group_mask = lax.dynamic_slice_in_dim(pattern, col_id * n_rows, n_rows, 1).astype(BF)
    panels = lower_panel[:, 0] * group_mask[:, :, None, None]
    own_mask = lax.dynamic_index_in_dim(group_mask, row_id, 1, keepdims=False).astype(F32)

    slabs = panels.reshape(supers, n_rows * piece, width)
    partial = jnp.stack([dot(known, slabs[k]).astype(BF).reshape(n_cols, piece, width) for k in range(supers)], 1)
    product = scatter_cols(partial)

    start = [top_diag] + [diag_inverse[k] for k in reversed(range(1, supers))]
    level_of = lambda c: supers - c
    mine = jnp.zeros((share, width), F32)
    for i, s in enumerate(start):
        mine = jnp.where(col_id % len(start) == i, s, mine) if n_cols <= len(start) else jnp.where(col_id == i, s, mine)
    joined = jnp.concatenate([mine.astype(BF), top_cols.reshape(piece, width)], 0)
    gathered, order = gather_rows(joined)
    shares = gathered[:, :share].reshape(width, width)
    tops = gathered[:, share:].reshape(n_rows * piece, width)
    order = jnp.stack([jnp.asarray(o, jnp.int32) for o in order])
    panel_rel = [p[order].reshape(n_rows * piece, width) for p in panels]
    own_rows = (lax.broadcasted_iota(jnp.int32, (share, width), 1) == row_id * share + lax.broadcasted_iota(jnp.int32, (share, width), 0)).astype(BF)
    stacks = [own_rows]
    for k in range(supers):
        stacks.append(jnp.concatenate([dot_nt(stacks[k], chain_panel[k]).astype(BF), own_rows], 0))
    begins = []
    for k in range(supers + 1):
        rel = stacks[k].reshape(-1, n_rows, share)[:, order].reshape(-1, width)
        begins.append(dot(rel, shares))
    reach = [dot_nt(stacks[k], panel_rel[k]).astype(BF) for k in range(supers)]

    prev = top_cols.reshape(piece, width)
    cols_list = [None] * supers
    for k in reversed(range(supers)):
        carried = dot(prev, chain_panel[k])
        prev = (-(product[k] + carried) * own_mask[k]).astype(BF)
        cols_list[k] = prev
    cols_out = jnp.stack(cols_list)
    all_cols, _ = gather_rows(cols_out)
    slab_cols = [all_cols[:, k].reshape(n_rows * piece, width) for k in range(supers)] + [tops]

    acc = jnp.where(col_id == 0, begins[supers], 0.0)
    diag_list = [None] * supers
    sub_list = [None] * supers
    for k in reversed(range(supers)):
        across = dot_nt(stacks[k + 1], slab_cols[k + 1]).astype(BF)
        full = dot(acc.astype(BF), chain_panel[k]) + dot(across, panel_rel[k])
        sub_list[k] = -full[(k + 1) * share:]
        acc = full[: (k + 1) * share] - dot(reach[k], slab_cols[k])
        diag_list[k] = acc[k * share :]
        if k:
            acc = acc + jnp.where(col_id == level_of(k), begins[k], 0.0)
    done = jnp.stack(diag_list + sub_list)
    if share % n_cols == 0:
        part = share // n_cols
        pieces = jnp.swapaxes(done.astype(BF).reshape(2 * supers, n_cols, part, width), 0, 1)
        summed = gather_cols(scatter_cols(pieces).astype(BF))
        summed = jnp.swapaxes(summed, 0, 1).reshape(2 * supers, share, width)
    else:
        summed = lax.psum(done.astype(BF), "cols")
    summed = summed.astype(F32)
    return (
        cols_out.reshape(supers, 1, 1, piece, width),
        diag_inverse + summed[:supers],
        summed[supers:],
    )


def fetch(source, into, sem):
    copy = pltpu.make_async_copy(source, into, sem)
    copy.start()
    return copy


def first_kernel(n_cols, n_rows, g_any, m_any, pattern_any, *refs):
    panel_ref, mask_ref = refs[:2]
    piece_refs = refs[2 : 2 + n_cols]
    g_ref, m_ref, pattern_ref, sems = refs[2 + n_cols :]
    col, row = lax.axis_index("cols"), lax.axis_index("rows")
    supers, _, piece, _ = m_ref.shape
    pattern_copy = fetch(pattern_any, pattern_ref, sems.at[0])
    panel_copies = [fetch(m_any.at[k], m_ref.at[k], sems.at[1 + k]) for k in range(supers)]
    g_copy = fetch(g_any, g_ref, sems.at[1 + supers])
    pattern_copy.wait()
    for k in range(supers):
        mask_ref[k] = jnp.full(mask_ref.shape[1:], pattern_ref[k, col * n_rows + row].astype(F32))
        panel_copies[k].wait()
        if k == 0:
            g_copy.wait()
        for r in range(n_rows):
            on = pattern_ref[k, col * n_rows + r].astype(F32)
            panel_ref[k, pl.ds(r * piece, piece)] = (m_ref[k, r].astype(F32) * on).astype(BF)
        for j, out in enumerate(piece_refs):
            out[k] = dot(g_ref[col ^ j], panel_ref[k]).astype(BF)


def chain_kernel(l_ref, joined_ref, mask_ref, own_ref, *refs):
    *got_refs, cols_ref, copy_ref = refs
    supers, piece, _ = own_ref.shape
    prev = joined_ref[pl.ds(joined_ref.shape[0] - piece, piece)]
    for k in reversed(range(supers)):
        total = own_ref[k].astype(F32)
        for got in got_refs:
            total = total + got[k].astype(F32)
        total = total + dot(prev, l_ref[k])
        prev = (-(total * mask_ref[k, pl.ds(0, 1)])).astype(BF)
        cols_ref[k] = prev
        copy_ref[k] = prev


def place(refs, order, write):
    me = lax.axis_index("rows")
    for ref, offset in zip(refs, order):
        write(me ^ offset, ref)


def ready_kernel(n_cols, n_rows, l_any, diag_any, top_any, tops_any, panel_ref, *refs):
    l_ref, stacks_ref, reach_ref, joined_ref, begin_ref, tops_ref, sems = refs
    supers, width, _ = l_ref.shape
    share, piece = width // n_rows, tops_ref.shape[0]
    col, row = lax.axis_index("cols"), lax.axis_index("rows")
    copies = [fetch(l_any.at[k], l_ref.at[k], sems.at[k]) for k in range(supers)]
    tops_copy = fetch(tops_any, tops_ref, sems.at[supers])

    @pl.when(col == 0)
    def _():
        fetch(top_any, begin_ref, sems.at[supers + 1]).wait()

    @pl.when(jnp.logical_and(col > 0, col < supers))
    def _():
        fetch(diag_any.at[jnp.clip(supers - col, 1, supers - 1)], begin_ref, sems.at[supers + 1]).wait()

    @pl.when(col >= supers)
    def _():
        begin_ref[...] = jnp.zeros_like(begin_ref)

    tops_copy.wait()
    joined_ref[pl.ds(0, share)] = begin_ref[...].astype(BF)
    joined_ref[pl.ds(share, piece)] = tops_ref[...]
    lane = lax.broadcasted_iota(jnp.int32, (share, width), 1)
    sub = lax.broadcasted_iota(jnp.int32, (share, width), 0)
    unit = jnp.where(lane == row * share + sub, 1.0, 0.0).astype(BF)
    stacks_ref[...] = jnp.zeros_like(stacks_ref)
    stacks_ref[0, pl.ds(0, share)] = unit
    stack, at = unit, 0
    for k in range(supers):
        reach_ref[pl.ds(at, (k + 1) * share)] = dot_nt(stack, panel_ref[k]).astype(BF)
        at += (k + 1) * share
        copies[k].wait()
        stack = jnp.concatenate([dot_nt(stack, l_ref[k]).astype(BF), unit], 0)
        stacks_ref[k + 1, pl.ds(0, (k + 2) * share)] = stack


def place(refs, order, write):
    me = lax.axis_index("rows")
    for ref, offset in zip(refs, order):
        write(me ^ offset, ref)


def begin_kernel(n_cols, n_rows, order, l_ref, panel_ref, stacks_ref, *refs):
    got = refs[: len(order)]
    begin_ref, ahead_ref, x_ref, y_ref = refs[len(order) :]
    supers, width, _ = l_ref.shape
    share, piece = width // n_rows, y_ref.shape[0] // n_rows
    col = lax.axis_index("cols")

    def write(at, ref):
        x_ref[pl.ds(pl.multiple_of(at * share, share), share)] = ref[pl.ds(0, share)]
        y_ref[pl.ds(pl.multiple_of(at * piece, piece), piece)] = ref[pl.ds(share, piece)]

    place(got, order, write)
    begin = dot(stacks_ref[jnp.maximum(supers - col, 0)], x_ref[...])
    begin_ref[...] = begin
    first = jnp.where(col == 0, begin, 0.0).astype(BF)
    across = dot_nt(stacks_ref[supers], y_ref[...]).astype(BF)
    ahead_ref[...] = dot(first, l_ref[supers - 1]) + dot(across, panel_ref[supers - 1])


def rows_kernel(n_cols, n_rows, order, l_ref, panel_ref, stacks_ref, reach_ref, begin_ref, ahead_ref, *refs):
    got = refs[: len(order)]
    pieces = refs[len(order) : len(order) + n_cols]
    y_ref, done_ref = refs[len(order) + n_cols :]
    supers, width, _ = l_ref.shape
    share = width // n_rows
    piece = y_ref.shape[1] // n_rows
    part = share // n_cols
    col = lax.axis_index("cols")

    def write(at, ref):
        for k in range(supers):
            y_ref[k, pl.ds(pl.multiple_of(at * piece, piece), piece)] = ref[k]

    place(got, order, write)
    full = ahead_ref[...]
    reach_at = sum((k + 1) * share for k in range(supers))
    for k in reversed(range(supers)):
        here = (k + 1) * share
        if k < supers - 1:
            across = dot_nt(stacks_ref[k + 1, pl.ds(0, here + share)], y_ref[k + 1]).astype(BF)
            full = dot(acc.astype(BF), l_ref[k]) + dot(across, panel_ref[k])
        reach_at -= here
        acc = full[:here] - dot(reach_ref[pl.ds(reach_at, here)], y_ref[k])
        done_ref[supers + k] = -full[here:]
        done_ref[k] = acc[k * share :]
        if k:
            acc = acc + jnp.where(col == supers - k, begin_ref[pl.ds(0, here)], 0.0)
    for j, out in enumerate(pieces):
        at = pl.multiple_of((col ^ j) * part, part)
        for i in range(2 * supers):
            out[i] = done_ref[i, pl.ds(at, part)].astype(BF)


def sum_kernel(own_ref, *refs):
    *got_refs, out_ref = refs
    for i in range(own_ref.shape[0]):
        total = own_ref[i].astype(F32)
        for got in got_refs:
            total = total + got[i].astype(F32)
        out_ref[i] = total.astype(BF)


def last_kernel(n_cols, diag_ref, *refs):
    *got_refs, diag_out, sub_out = refs
    supers = diag_ref.shape[0]
    part = got_refs[0].shape[1]
    col = lax.axis_index("cols")
    for j, got in enumerate(got_refs):
        rows = pl.ds(pl.multiple_of((col ^ j) * part, part), part)
        for k in range(supers):
            diag_out[k, rows] = diag_ref[k, rows] + got[k].astype(F32)
            sub_out[k, rows] = got[supers + k].astype(F32)


def call(kernel, outs, *args, scratch=(), away=(), flops=0, moved=0):
    vmem, hbm = pl.BlockSpec(memory_space=pltpu.VMEM), pl.BlockSpec(memory_space=pltpu.HBM)
    return pl.pallas_call(
        kernel,
        out_shape=tuple(jax.ShapeDtypeStruct(s, d) for s, d in outs),
        in_specs=[hbm if i in away else vmem for i in range(len(args))],
        out_specs=tuple(vmem for _ in outs),
        scratch_shapes=scratch,
        compiler_params=pltpu.CompilerParams(vmem_limit_bytes=VMEM_BYTES),
        cost_estimate=pl.CostEstimate(flops=flops, bytes_accessed=moved, transcendentals=0),
    )(*[pltpu.with_memory_space_constraint(a, pltpu.HBM) if i in away else a for i, a in enumerate(args)])


def exchange_rows(x):
    near = [x] + [hop(x, "rows", j) for j in ROW_ORDER[1:4]]
    return near + [hop(p, "rows", 1) for p in near]


def local(known_inverse, lower_panel, chain_panel, diag_inverse, top_cols, top_diag, pattern):
    n_rows = lax.axis_size("rows")
    n_cols = lax.axis_size("cols")
    supers = lower_panel.shape[0]
    piece = known_inverse.shape[2]
    width = lower_panel.shape[-1]
    share = width // n_rows
    if n_rows != len(ROW_ORDER) or not pow2(n_cols) or n_cols < supers or share % (16 * n_cols) or piece % 16:
        return general(known_inverse, lower_panel, chain_panel, diag_inverse, top_cols, top_diag, pattern)
    known = known_inverse[:, 0]
    tops = top_cols[0, 0]
    block = n_rows * piece
    ways = range(1, n_cols)
    rows_of = [(k + 1) * share for k in range(supers + 1)]
    panel, mask, own, *sent = call(
        functools.partial(first_kernel, n_cols, n_rows),
        [((supers, block, width), BF), ((supers, 8, width), F32)] + [((supers, piece, width), BF)] * n_cols,
        known, lower_panel[:, 0], pattern, away=range(3),
        scratch=[
            pltpu.VMEM(known.shape, BF), pltpu.VMEM((supers, n_rows, piece, width), BF),
            pltpu.SMEM(pattern.shape, jnp.int32), pltpu.SemaphoreType.DMA((2 + supers,)),
        ],
        flops=2 * known.size * supers * width, moved=4 * block * width * supers,
    )
    got = [hop(sent[j - 1], "cols", j) for j in reversed(ways)]
    links, stacks, reach, joined = call(
        functools.partial(ready_kernel, n_cols, n_rows),
        [(chain_panel.shape, BF), ((supers + 1, rows_of[supers], width), BF), ((sum(rows_of[:supers]), block), BF), ((share + piece, width), BF)],
        chain_panel, diag_inverse, top_diag, tops, panel, away=range(4),
        scratch=[pltpu.VMEM((share, width), F32), pltpu.VMEM((piece, width), BF), pltpu.SemaphoreType.DMA((supers + 2,))],
        flops=2 * 12 * share * width * width, moved=4 * width * width * supers,
    )
    begin, ahead = call(
        functools.partial(begin_kernel, n_cols, n_rows, ROW_ORDER),
        [((rows_of[supers], width), F32)] * 2,
        links, panel, stacks, *exchange_rows(joined),
        scratch=[pltpu.VMEM((width, width), BF), pltpu.VMEM((block, width), BF)],
        flops=2 * 15 * share * width * width, moved=4 * width * width,
    )
    cols, cols_out = call(
        chain_kernel,
        [((supers, piece, width), BF)] * 2,
        links, joined, mask, own, *got,
        flops=2 * piece * width * width * supers, moved=2 * width * width * supers,
    )
    pieces = call(
        functools.partial(rows_kernel, n_cols, n_rows, ROW_ORDER),
        [((2 * supers, share // n_cols, width), BF)] * n_cols,
        links, panel, stacks, reach, begin, ahead, *exchange_rows(cols),
        scratch=[pltpu.VMEM((supers, block, width), BF), pltpu.VMEM((2 * supers, share, width), F32)],
        flops=2 * 20 * share * width * width, moved=4 * width * width * supers,
    )
    got = [hop(pieces[j], "cols", j) for j in reversed(ways)]
    (summed,) = call(sum_kernel, [(pieces[0].shape, BF)], pieces[0], *got)
    there = {j: hop(summed, "cols", j) for j in reversed(ways)}
    diag, sub = call(
        functools.partial(last_kernel, n_cols),
        [(diag_inverse.shape, F32)] * 2,
        diag_inverse, summed, *[there[j] for j in ways],
    )
    return cols_out.reshape(supers, 1, 1, piece, width), diag, sub


def solution(mesh):
    in_specs = (
        P(None, "rows", None, "cols"),
        P(None, "cols", None, None, None),
        P(),
        P(None, "rows", None),
        P("cols", "rows", None, None),
        P("rows", None),
        P(),
    )
    out_specs = (P(None, "cols", "rows", None, None), P(None, "rows", None), P(None, "rows", None))
    return jax.shard_map(local, mesh=mesh, in_specs=in_specs, out_specs=out_specs, check_vma=False)
```

```python
import functools

import jax
import jax.numpy as jnp
from jax import lax
from jax.experimental import pallas as pl
from jax.experimental.pallas import tpu as pltpu
from jax.sharding import PartitionSpec as P

BF = jnp.bfloat16
F32 = jnp.float32
ROW_ORDER = (0, 6, 4, 2, 1, 7, 5, 3)
VMEM_BYTES = 32 << 20
AG_ORDER = (1, 2, 3)


def dot(a, b):
    return jnp.dot(a, b, preferred_element_type=F32)


def dot_nt(a, b):
    return lax.dot_general(a, b, (((1,), (1,)), ((), ())), preferred_element_type=F32)


def pow2(n):
    return n & (n - 1) == 0


def target(i, j, n):
    return i ^ j if pow2(n) else (i + j) % n


def source(i, j, n):
    return i ^ j if pow2(n) else (i - j) % n


def hop(x, axis, j):
    n = lax.axis_size(axis)
    return lax.ppermute(x, axis, [(i, target(i, j, n)) for i in range(n)])


def gather_rows(x):
    n = lax.axis_size("rows")
    me = lax.axis_index("rows")
    if n == 8:
        parts = [x] + [hop(x, "rows", j) for j in (6, 4, 2)]
        offsets = [0, 6, 4, 2]
        here = jnp.stack(parts)
        there = hop(here, "rows", 1)
        whole = jnp.concatenate([here, there], 0)
        offsets = offsets + [o ^ 1 for o in offsets]
        return whole, [source(me, o, n) for o in offsets]
    if pow2(n):
        whole, offsets, bit = x[None], [0], n // 2
        while bit:
            whole = jnp.concatenate([whole, hop(whole, "rows", bit)], 0)
            offsets = offsets + [o ^ bit for o in offsets]
            bit //= 2
        return whole, [source(me, o, n) for o in offsets]
    return lax.all_gather(x, "rows"), list(range(n))


def scatter_cols(pieces):
    n = lax.axis_size("cols")
    me = lax.axis_index("cols")
    total = lax.dynamic_index_in_dim(pieces, me, 0, False).astype(F32)
    for j in reversed(range(1, n)):
        sent = lax.dynamic_index_in_dim(pieces, target(me, j, n), 0, False)
        total = total + hop(sent, "cols", j).astype(F32)
    return total


def gather_cols(x):
    n = lax.axis_size("cols")
    me = lax.axis_index("cols")
    whole = jnp.zeros((n,) + x.shape, x.dtype)
    got = [(me, x)] + [(source(me, j, n), hop(x, "cols", j)) for j in reversed(range(1, n))]
    for at, piece in got:
        whole = lax.dynamic_update_index_in_dim(whole, piece, at, 0)
    return whole


def general(known_inverse, lower_panel, chain_panel, diag_inverse, top_cols, top_diag, pattern):
    n_rows = lax.axis_size("rows")
    n_cols = lax.axis_size("cols")
    row_id = lax.axis_index("rows")
    col_id = lax.axis_index("cols")
    supers = lower_panel.shape[0]
    piece = known_inverse.shape[2]
    width = lower_panel.shape[-1]
    share = width // n_rows
    known = known_inverse.reshape(n_cols * piece, -1)
    group_mask = lax.dynamic_slice_in_dim(pattern, col_id * n_rows, n_rows, 1).astype(BF)
    panels = lower_panel[:, 0] * group_mask[:, :, None, None]
    own_mask = lax.dynamic_index_in_dim(group_mask, row_id, 1, keepdims=False).astype(F32)

    slabs = panels.reshape(supers, n_rows * piece, width)
    partial = jnp.stack([dot(known, slabs[k]).astype(BF).reshape(n_cols, piece, width) for k in range(supers)], 1)
    product = scatter_cols(partial)

    start = [top_diag] + [diag_inverse[k] for k in reversed(range(1, supers))]
    level_of = lambda c: supers - c
    mine = jnp.zeros((share, width), F32)
    for i, s in enumerate(start):
        mine = jnp.where(col_id % len(start) == i, s, mine) if n_cols <= len(start) else jnp.where(col_id == i, s, mine)
    joined = jnp.concatenate([mine.astype(BF), top_cols.reshape(piece, width)], 0)
    gathered, order = gather_rows(joined)
    shares = gathered[:, :share].reshape(width, width)
    tops = gathered[:, share:].reshape(n_rows * piece, width)
    order = jnp.stack([jnp.asarray(o, jnp.int32) for o in order])
    panel_rel = [p[order].reshape(n_rows * piece, width) for p in panels]
    own_rows = (lax.broadcasted_iota(jnp.int32, (share, width), 1) == row_id * share + lax.broadcasted_iota(jnp.int32, (share, width), 0)).astype(BF)
    stacks = [own_rows]
    for k in range(supers):
        stacks.append(jnp.concatenate([dot_nt(stacks[k], chain_panel[k]).astype(BF), own_rows], 0))
    begins = []
    for k in range(supers + 1):
        rel = stacks[k].reshape(-1, n_rows, share)[:, order].reshape(-1, width)
        begins.append(dot(rel, shares))
    reach = [dot_nt(stacks[k], panel_rel[k]).astype(BF) for k in range(supers)]

    prev = top_cols.reshape(piece, width)
    cols_list = [None] * supers
    for k in reversed(range(supers)):
        carried = dot(prev, chain_panel[k])
        prev = (-(product[k] + carried) * own_mask[k]).astype(BF)
        cols_list[k] = prev
    cols_out = jnp.stack(cols_list)
    all_cols, _ = gather_rows(cols_out)
    slab_cols = [all_cols[:, k].reshape(n_rows * piece, width) for k in range(supers)] + [tops]

    acc = jnp.where(col_id == 0, begins[supers], 0.0)
    diag_list = [None] * supers
    sub_list = [None] * supers
    for k in reversed(range(supers)):
        across = dot_nt(stacks[k + 1], slab_cols[k + 1]).astype(BF)
        full = dot(acc.astype(BF), chain_panel[k]) + dot(across, panel_rel[k])
        sub_list[k] = -full[(k + 1) * share:]
        acc = full[: (k + 1) * share] - dot(reach[k], slab_cols[k])
        diag_list[k] = acc[k * share :]
        if k:
            acc = acc + jnp.where(col_id == level_of(k), begins[k], 0.0)
    done = jnp.stack(diag_list + sub_list)
    if share % n_cols == 0:
        part = share // n_cols
        pieces = jnp.swapaxes(done.astype(BF).reshape(2 * supers, n_cols, part, width), 0, 1)
        summed = gather_cols(scatter_cols(pieces).astype(BF))
        summed = jnp.swapaxes(summed, 0, 1).reshape(2 * supers, share, width)
    else:
        summed = lax.psum(done.astype(BF), "cols")
    summed = summed.astype(F32)
    return (
        cols_out.reshape(supers, 1, 1, piece, width),
        diag_inverse + summed[:supers],
        summed[supers:],
    )


def fetch(source, into, sem):
    copy = pltpu.make_async_copy(source, into, sem)
    copy.start()
    return copy


def first_kernel(n_cols, n_rows, g_any, m_any, pattern_any, *refs):
    panel_ref, mask_ref = refs[:2]
    piece_refs = refs[2 : 2 + n_cols]
    g_ref, m_ref, pattern_ref, sems = refs[2 + n_cols :]
    col, row = lax.axis_index("cols"), lax.axis_index("rows")
    supers, _, piece, _ = m_ref.shape
    pattern_copy = fetch(pattern_any, pattern_ref, sems.at[0])
    g_copies = [fetch(g_any.at[col ^ j], g_ref.at[pl.ds(j * piece, piece)], sems.at[1 + supers + j]) for j in range(n_cols)]
    panel_copies = [fetch(m_any.at[k], m_ref.at[k], sems.at[1 + k]) for k in range(supers)]
    pattern_copy.wait()
    for copy in g_copies:
        copy.wait()
    for k in range(supers):
        mask_ref[k] = jnp.full(mask_ref.shape[1:], pattern_ref[k, col * n_rows + row].astype(F32))
        panel_copies[k].wait()
        for r in range(n_rows):
            on = pattern_ref[k, col * n_rows + r] != 0
            panel_ref[k, pl.ds(r * piece, piece)] = jnp.where(on, m_ref[k, r], jnp.zeros_like(m_ref[k, r]))
        product = dot(g_ref[...], panel_ref[k]).astype(BF)
        for j, out in enumerate(piece_refs):
            out[k] = product[j * piece : (j + 1) * piece]


def chain_kernel(l_ref, joined_ref, mask_ref, own_ref, *refs):
    *got_refs, cols_ref, copy_ref = refs
    supers, piece, _ = own_ref.shape
    prev = joined_ref[pl.ds(joined_ref.shape[0] - piece, piece)]
    for k in reversed(range(supers)):
        total = own_ref[k].astype(F32)
        for got in got_refs:
            total = total + got[k].astype(F32)
        total = total + dot(prev, l_ref[k])
        prev = (-(total * mask_ref[k, pl.ds(0, 1)])).astype(BF)
        cols_ref[k] = prev
        copy_ref[k] = prev


def place(refs, order, write):
    me = lax.axis_index("rows")
    for ref, offset in zip(refs, order):
        write(me ^ offset, ref)


def ready_kernel(n_cols, n_rows, l_any, diag_any, top_any, tops_any, panel_ref, *refs):
    l_ref, stacks_ref, reach_ref, joined_ref, begin_ref, tops_ref, sems = refs
    supers, width, _ = l_ref.shape
    share, piece = width // n_rows, tops_ref.shape[0]
    col, row = lax.axis_index("cols"), lax.axis_index("rows")
    copies = [fetch(l_any.at[k], l_ref.at[k], sems.at[k]) for k in range(supers)]
    tops_copy = fetch(tops_any, tops_ref, sems.at[supers])

    @pl.when(col == 0)
    def _():
        fetch(top_any, begin_ref, sems.at[supers + 1]).wait()

    @pl.when(jnp.logical_and(col > 0, col < supers))
    def _():
        fetch(diag_any.at[jnp.clip(supers - col, 1, supers - 1)], begin_ref, sems.at[supers + 1]).wait()

    @pl.when(col >= supers)
    def _():
        begin_ref[...] = jnp.zeros_like(begin_ref)

    tops_copy.wait()
    joined_ref[pl.ds(0, share)] = begin_ref[...].astype(BF)
    joined_ref[pl.ds(share, piece)] = tops_ref[...]
    lane = lax.broadcasted_iota(jnp.int32, (share, width), 1)
    sub = lax.broadcasted_iota(jnp.int32, (share, width), 0)
    unit = jnp.where(lane == row * share + sub, 1.0, 0.0).astype(BF)
    stacks_ref[...] = jnp.zeros_like(stacks_ref)
    stacks_ref[0, pl.ds(0, share)] = unit
    stack, at = unit, 0
    for k in range(supers):
        reach_ref[pl.ds(at, (k + 1) * share)] = dot_nt(stack, panel_ref[k]).astype(BF)
        at += (k + 1) * share
        copies[k].wait()
        stack = jnp.concatenate([dot_nt(stack, l_ref[k]).astype(BF), unit], 0)
        stacks_ref[k + 1, pl.ds(0, (k + 2) * share)] = stack


def place(refs, order, write):
    me = lax.axis_index("rows")
    for ref, offset in zip(refs, order):
        write(me ^ offset, ref)


def begin_kernel(n_cols, n_rows, order, l_ref, panel_ref, stacks_ref, *refs):
    got = refs[: len(order)]
    begin_ref, ahead_ref, x_ref, y_ref = refs[len(order) :]
    supers, width, _ = l_ref.shape
    share, piece = width // n_rows, y_ref.shape[0] // n_rows
    col = lax.axis_index("cols")

    def write(at, ref):
        x_ref[pl.ds(pl.multiple_of(at * share, share), share)] = ref[pl.ds(0, share)]
        y_ref[pl.ds(pl.multiple_of(at * piece, piece), piece)] = ref[pl.ds(share, piece)]

    place(got, order, write)
    begin = dot(stacks_ref[jnp.maximum(supers - col, 0)], x_ref[...])
    begin_ref[...] = begin
    first = jnp.where(col == 0, begin, 0.0).astype(BF)
    across = dot_nt(stacks_ref[supers], y_ref[...]).astype(BF)
    ahead_ref[...] = dot(first, l_ref[supers - 1]) + dot(across, panel_ref[supers - 1])


def rows_kernel(n_cols, n_rows, order, levels, last, l_ref, panel_ref, stacks_ref, reach_ref, begin_ref, from_ref, *refs):
    got, refs = refs[: len(order)], refs[len(order) :]
    pieces, refs = refs[:n_cols], refs[n_cols:]
    *acc_refs, y_ref, done_ref = refs
    supers, width, _ = l_ref.shape
    share = width // n_rows
    piece = y_ref.shape[1] // n_rows
    part = share // n_cols
    col = lax.axis_index("cols")
    top = levels[0] == supers - 1

    def write(at, ref):
        for k in range(levels[-1], levels[0] + (1 if top else 2)):
            y_ref[k, pl.ds(pl.multiple_of(at * piece, piece), piece)] = ref[k]

    place(got, order, write)
    acc = from_ref[...]
    for i, k in enumerate(levels):
        here = (k + 1) * share
        if k == supers - 1:
            full = acc
        else:
            across = dot_nt(stacks_ref[k + 1, pl.ds(0, here + share)], y_ref[k + 1]).astype(BF)
            full = dot(acc.astype(BF), l_ref[k]) + dot(across, panel_ref[k])
        acc = full[:here] - dot(reach_ref[pl.ds(sum((j + 1) * share for j in range(k)), here)], y_ref[k])
        done_ref[2 * i] = acc[k * share :].astype(BF)
        done_ref[2 * i + 1] = (-full[here:]).astype(BF)
        if k:
            acc = acc + jnp.where(col == supers - k, begin_ref[pl.ds(0, here)], 0.0)
    if not last:
        acc_refs[0][...] = acc
    for j, out in enumerate(pieces):
        out[...] = done_ref[:, pl.ds(pl.multiple_of((col ^ j) * part, part), part)]


def sum_kernel(own_ref, *refs):
    *got_refs, out_ref = refs
    for i in range(own_ref.shape[0]):
        total = own_ref[i].astype(F32)
        for got in got_refs:
            total = total + got[i].astype(F32)
        out_ref[i] = total.astype(BF)


def last_kernel(n_cols, offsets, levels, diag_ref, *refs):
    got_refs = refs[:n_cols]
    diag_out, sub_out, done_ref, sems = refs[-4:]
    part = got_refs[0].shape[1]
    col = lax.axis_index("cols")
    copies = []
    for i, k in enumerate(levels):
        for j, got in zip(offsets, got_refs):
            rows = pl.ds(pl.multiple_of((col ^ j) * part, part), part)
            done_ref[2 * i, rows] = diag_ref[k, rows] + got[2 * i].astype(F32)
            done_ref[2 * i + 1, rows] = got[2 * i + 1].astype(F32)
        copies.append(fetch(done_ref.at[2 * i], diag_out.at[k], sems.at[2 * i]))
        copies.append(fetch(done_ref.at[2 * i + 1], sub_out.at[k], sems.at[2 * i + 1]))
    for copy in copies:
        copy.wait()


def call(kernel, outs, *args, scratch=(), away=(), out_away=False, aliases=None, flops=0, moved=0):
    vmem, hbm = pl.BlockSpec(memory_space=pltpu.VMEM), pl.BlockSpec(memory_space=pltpu.HBM)
    return pl.pallas_call(
        kernel,
        out_shape=tuple(jax.ShapeDtypeStruct(s, d) for s, d in outs),
        in_specs=[hbm if i in away else vmem for i in range(len(args))],
        out_specs=tuple(hbm if out_away else vmem for _ in outs),
        input_output_aliases=aliases or {},
        scratch_shapes=scratch,
        compiler_params=pltpu.CompilerParams(vmem_limit_bytes=VMEM_BYTES),
        cost_estimate=pl.CostEstimate(flops=flops, bytes_accessed=moved, transcendentals=0),
    )(*[pltpu.with_memory_space_constraint(a, pltpu.HBM) if i in away else a for i, a in enumerate(args)])


def exchange_rows(x):
    near = [x] + [hop(x, "rows", j) for j in ROW_ORDER[1:4]]
    return near + [hop(p, "rows", 1) for p in near]


def local(known_inverse, lower_panel, chain_panel, diag_inverse, top_cols, top_diag, pattern):
    n_rows = lax.axis_size("rows")
    n_cols = lax.axis_size("cols")
    supers = lower_panel.shape[0]
    piece = known_inverse.shape[2]
    width = lower_panel.shape[-1]
    share = width // n_rows
    if n_rows != len(ROW_ORDER) or not pow2(n_cols) or n_cols < supers or share % (16 * n_cols) or piece % 16:
        return general(known_inverse, lower_panel, chain_panel, diag_inverse, top_cols, top_diag, pattern)
    known = known_inverse[:, 0]
    tops = top_cols[0, 0]
    block = n_rows * piece
    ways = range(1, n_cols)
    rows_of = [(k + 1) * share for k in range(supers + 1)]
    panel, mask, own, *sent = call(
        functools.partial(first_kernel, n_cols, n_rows),
        [((supers, block, width), BF), ((supers, 8, width), F32)] + [((supers, piece, width), BF)] * n_cols,
        known, lower_panel[:, 0], pattern, away=range(3),
        scratch=[
            pltpu.VMEM((n_cols * piece, block), BF), pltpu.VMEM((supers, n_rows, piece, width), BF),
            pltpu.SMEM(pattern.shape, jnp.int32), pltpu.SemaphoreType.DMA((1 + supers + n_cols,)),
        ],
        flops=2 * known.size * supers * width, moved=4 * block * width * supers,
    )
    got = [hop(sent[j - 1], "cols", j) for j in reversed(ways)]
    links, stacks, reach, joined = call(
        functools.partial(ready_kernel, n_cols, n_rows),
        [(chain_panel.shape, BF), ((supers + 1, rows_of[supers], width), BF), ((sum(rows_of[:supers]), block), BF), ((share + piece, width), BF)],
        chain_panel, diag_inverse, top_diag, tops, panel, away=range(4),
        scratch=[pltpu.VMEM((share, width), F32), pltpu.VMEM((piece, width), BF), pltpu.SemaphoreType.DMA((supers + 2,))],
        flops=2 * 12 * share * width * width, moved=4 * width * width * supers,
    )
    begin, ahead = call(
        functools.partial(begin_kernel, n_cols, n_rows, ROW_ORDER),
        [((rows_of[supers], width), F32)] * 2,
        links, panel, stacks, *exchange_rows(joined),
        scratch=[pltpu.VMEM((width, width), BF), pltpu.VMEM((block, width), BF)],
        flops=2 * 15 * share * width * width, moved=4 * width * width,
    )
    cols, cols_out = call(
        chain_kernel,
        [((supers, piece, width), BF)] * 2,
        links, joined, mask, own, *got,
        flops=2 * piece * width * width * supers, moved=2 * width * width * supers,
    )
    arrived = exchange_rows(cols)
    split = supers // 2
    groups = [tuple(reversed(range(split, supers))), tuple(reversed(range(split)))]
    state, parts = ahead, []
    for levels in groups:
        last = levels[-1] == 0
        count = 2 * len(levels)
        *pieces, state = call(
            functools.partial(rows_kernel, n_cols, n_rows, ROW_ORDER, levels, last),
            [((count, share // n_cols, width), BF)] * n_cols + ([] if last else [((levels[-1] * share + share, width), F32)]),
            links, panel, stacks, reach, begin, state, *arrived,
            scratch=[pltpu.VMEM((supers, block, width), BF), pltpu.VMEM((count, share, width), BF)],
            flops=2 * 10 * share * width * width, moved=4 * width * width * supers,
        ) + ((None,) if last else ())
        parts.append((levels, pieces))
    sums = []
    for levels, pieces in parts:
        got = [hop(pieces[j], "cols", j) for j in reversed(ways)]
        sums.append((levels, call(sum_kernel, [(pieces[0].shape, BF)], pieces[0], *got)[0]))
    filled = ()
    for levels, summed in sums:
        offsets = [0] + [j for j in AG_ORDER if j < n_cols]
        got = [summed] + [hop(summed, "cols", j) for j in offsets[1:]]
        filled = call(
            functools.partial(last_kernel, n_cols, offsets, levels),
            [(diag_inverse.shape, F32)] * 2,
            diag_inverse, *got, *filled, away=range(1 + n_cols, 1 + n_cols + len(filled)), out_away=True,
            aliases={1 + n_cols + i: i for i in range(len(filled))},
            scratch=[pltpu.VMEM((2 * len(levels), share, width), F32), pltpu.SemaphoreType.DMA((2 * len(levels),))],
        )
    diag, sub = filled
    return cols_out.reshape(supers, 1, 1, piece, width), diag, sub


def solution(mesh):
    in_specs = (
        P(None, "rows", None, "cols"),
        P(None, "cols", None, None, None),
        P(),
        P(None, "rows", None),
        P("cols", "rows", None, None),
        P("rows", None),
        P(),
    )
    out_specs = (P(None, "cols", "rows", None, None), P(None, "rows", None), P(None, "rows", None))
    return jax.shard_map(local, mesh=mesh, in_specs=in_specs, out_specs=out_specs, check_vma=False)
```

```python
import functools

import jax
import jax.numpy as jnp
from jax import lax
from jax.experimental import pallas as pl
from jax.experimental.pallas import tpu as pltpu
from jax.sharding import PartitionSpec as P

BF = jnp.bfloat16
F32 = jnp.float32
ROW_ORDER = (0, 6, 4, 2, 1, 7, 5, 3)
VMEM_BYTES = 32 << 20
FIRST_ORDER = (3, 1, 2)
SUM_ORDER = (3, 2, 1)
LAST_ORDER = (1, 2, 3)


def dot(a, b):
    return jnp.dot(a, b, preferred_element_type=F32)


def dot_nt(a, b):
    return lax.dot_general(a, b, (((1,), (1,)), ((), ())), preferred_element_type=F32)


def pow2(n):
    return n & (n - 1) == 0


def target(i, j, n):
    return i ^ j if pow2(n) else (i + j) % n


def source(i, j, n):
    return i ^ j if pow2(n) else (i - j) % n


def hop(x, axis, j):
    n = lax.axis_size(axis)
    return lax.ppermute(x, axis, [(i, target(i, j, n)) for i in range(n)])


def gather_rows(x):
    n = lax.axis_size("rows")
    me = lax.axis_index("rows")
    if n == 8:
        parts = [x] + [hop(x, "rows", j) for j in (6, 4, 2)]
        offsets = [0, 6, 4, 2]
        here = jnp.stack(parts)
        there = hop(here, "rows", 1)
        whole = jnp.concatenate([here, there], 0)
        offsets = offsets + [o ^ 1 for o in offsets]
        return whole, [source(me, o, n) for o in offsets]
    if pow2(n):
        whole, offsets, bit = x[None], [0], n // 2
        while bit:
            whole = jnp.concatenate([whole, hop(whole, "rows", bit)], 0)
            offsets = offsets + [o ^ bit for o in offsets]
            bit //= 2
        return whole, [source(me, o, n) for o in offsets]
    return lax.all_gather(x, "rows"), list(range(n))


def scatter_cols(pieces):
    n = lax.axis_size("cols")
    me = lax.axis_index("cols")
    total = lax.dynamic_index_in_dim(pieces, me, 0, False).astype(F32)
    for j in reversed(range(1, n)):
        sent = lax.dynamic_index_in_dim(pieces, target(me, j, n), 0, False)
        total = total + hop(sent, "cols", j).astype(F32)
    return total


def gather_cols(x):
    n = lax.axis_size("cols")
    me = lax.axis_index("cols")
    whole = jnp.zeros((n,) + x.shape, x.dtype)
    got = [(me, x)] + [(source(me, j, n), hop(x, "cols", j)) for j in reversed(range(1, n))]
    for at, piece in got:
        whole = lax.dynamic_update_index_in_dim(whole, piece, at, 0)
    return whole


def general(known_inverse, lower_panel, chain_panel, diag_inverse, top_cols, top_diag, pattern):
    n_rows = lax.axis_size("rows")
    n_cols = lax.axis_size("cols")
    row_id = lax.axis_index("rows")
    col_id = lax.axis_index("cols")
    supers = lower_panel.shape[0]
    piece = known_inverse.shape[2]
    width = lower_panel.shape[-1]
    share = width // n_rows
    known = known_inverse.reshape(n_cols * piece, -1)
    group_mask = lax.dynamic_slice_in_dim(pattern, col_id * n_rows, n_rows, 1).astype(BF)
    panels = lower_panel[:, 0] * group_mask[:, :, None, None]
    own_mask = lax.dynamic_index_in_dim(group_mask, row_id, 1, keepdims=False).astype(F32)

    slabs = panels.reshape(supers, n_rows * piece, width)
    partial = jnp.stack([dot(known, slabs[k]).astype(BF).reshape(n_cols, piece, width) for k in range(supers)], 1)
    product = scatter_cols(partial)

    start = [top_diag] + [diag_inverse[k] for k in reversed(range(1, supers))]
    level_of = lambda c: supers - c
    mine = jnp.zeros((share, width), F32)
    for i, s in enumerate(start):
        mine = jnp.where(col_id % len(start) == i, s, mine) if n_cols <= len(start) else jnp.where(col_id == i, s, mine)
    joined = jnp.concatenate([mine.astype(BF), top_cols.reshape(piece, width)], 0)
    gathered, order = gather_rows(joined)
    shares = gathered[:, :share].reshape(width, width)
    tops = gathered[:, share:].reshape(n_rows * piece, width)
    order = jnp.stack([jnp.asarray(o, jnp.int32) for o in order])
    panel_rel = [p[order].reshape(n_rows * piece, width) for p in panels]
    own_rows = (lax.broadcasted_iota(jnp.int32, (share, width), 1) == row_id * share + lax.broadcasted_iota(jnp.int32, (share, width), 0)).astype(BF)
    stacks = [own_rows]
    for k in range(supers):
        stacks.append(jnp.concatenate([dot_nt(stacks[k], chain_panel[k]).astype(BF), own_rows], 0))
    begins = []
    for k in range(supers + 1):
        rel = stacks[k].reshape(-1, n_rows, share)[:, order].reshape(-1, width)
        begins.append(dot(rel, shares))
    reach = [dot_nt(stacks[k], panel_rel[k]).astype(BF) for k in range(supers)]

    prev = top_cols.reshape(piece, width)
    cols_list = [None] * supers
    for k in reversed(range(supers)):
        carried = dot(prev, chain_panel[k])
        prev = (-(product[k] + carried) * own_mask[k]).astype(BF)
        cols_list[k] = prev
    cols_out = jnp.stack(cols_list)
    all_cols, _ = gather_rows(cols_out)
    slab_cols = [all_cols[:, k].reshape(n_rows * piece, width) for k in range(supers)] + [tops]

    acc = jnp.where(col_id == 0, begins[supers], 0.0)
    diag_list = [None] * supers
    sub_list = [None] * supers
    for k in reversed(range(supers)):
        across = dot_nt(stacks[k + 1], slab_cols[k + 1]).astype(BF)
        full = dot(acc.astype(BF), chain_panel[k]) + dot(across, panel_rel[k])
        sub_list[k] = -full[(k + 1) * share:]
        acc = full[: (k + 1) * share] - dot(reach[k], slab_cols[k])
        diag_list[k] = acc[k * share :]
        if k:
            acc = acc + jnp.where(col_id == level_of(k), begins[k], 0.0)
    done = jnp.stack(diag_list + sub_list)
    if share % n_cols == 0:
        part = share // n_cols
        pieces = jnp.swapaxes(done.astype(BF).reshape(2 * supers, n_cols, part, width), 0, 1)
        summed = gather_cols(scatter_cols(pieces).astype(BF))
        summed = jnp.swapaxes(summed, 0, 1).reshape(2 * supers, share, width)
    else:
        summed = lax.psum(done.astype(BF), "cols")
    summed = summed.astype(F32)
    return (
        cols_out.reshape(supers, 1, 1, piece, width),
        diag_inverse + summed[:supers],
        summed[supers:],
    )


def fetch(source, into, sem):
    copy = pltpu.make_async_copy(source, into, sem)
    copy.start()
    return copy


def first_kernel(n_cols, n_rows, g_any, m_any, pattern_any, *refs):
    panel_ref, mask_ref = refs[:2]
    piece_refs = refs[2 : 2 + n_cols]
    g_ref, m_ref, pattern_ref, sems = refs[2 + n_cols :]
    col, row = lax.axis_index("cols"), lax.axis_index("rows")
    supers, _, piece, _ = m_ref.shape
    pattern_copy = fetch(pattern_any, pattern_ref, sems.at[0])
    g_copies = [fetch(g_any.at[col ^ j], g_ref.at[pl.ds(j * piece, piece)], sems.at[1 + supers + j]) for j in range(n_cols)]
    panel_copies = [fetch(m_any.at[k], m_ref.at[k], sems.at[1 + k]) for k in range(supers)]
    pattern_copy.wait()
    for copy in g_copies:
        copy.wait()
    for k in range(supers):
        mask_ref[k] = jnp.full(mask_ref.shape[1:], pattern_ref[k, col * n_rows + row].astype(F32))
        panel_copies[k].wait()
        for r in range(n_rows):
            on = pattern_ref[k, col * n_rows + r] != 0
            panel_ref[k, pl.ds(r * piece, piece)] = jnp.where(on, m_ref[k, r], jnp.zeros_like(m_ref[k, r]))
        product = dot(g_ref[...], panel_ref[k]).astype(BF)
        for j, out in enumerate(piece_refs):
            out[k] = product[j * piece : (j + 1) * piece]


def chain_kernel(l_ref, joined_ref, mask_ref, own_ref, *refs):
    *got_refs, cols_ref, copy_ref = refs
    supers, piece, _ = own_ref.shape
    prev = joined_ref[pl.ds(joined_ref.shape[0] - piece, piece)]
    for k in reversed(range(supers)):
        total = own_ref[k].astype(F32)
        for got in got_refs:
            total = total + got[k].astype(F32)
        total = total + dot(prev, l_ref[k])
        prev = (-(total * mask_ref[k, pl.ds(0, 1)])).astype(BF)
        cols_ref[k] = prev
        copy_ref[k] = prev


def place(refs, order, write):
    me = lax.axis_index("rows")
    for ref, offset in zip(refs, order):
        write(me ^ offset, ref)


def ready_kernel(n_cols, n_rows, l_any, diag_any, top_any, tops_any, panel_ref, *refs):
    l_ref, stacks_ref, reach_ref, joined_ref, begin_ref, tops_ref, sems = refs
    supers, width, _ = l_ref.shape
    share, piece = width // n_rows, tops_ref.shape[0]
    col, row = lax.axis_index("cols"), lax.axis_index("rows")
    copies = [fetch(l_any.at[k], l_ref.at[k], sems.at[k]) for k in range(supers)]
    tops_copy = fetch(tops_any, tops_ref, sems.at[supers])

    @pl.when(col == 0)
    def _():
        fetch(top_any, begin_ref, sems.at[supers + 1]).wait()

    @pl.when(jnp.logical_and(col > 0, col < supers))
    def _():
        fetch(diag_any.at[jnp.clip(supers - col, 1, supers - 1)], begin_ref, sems.at[supers + 1]).wait()

    @pl.when(col >= supers)
    def _():
        begin_ref[...] = jnp.zeros_like(begin_ref)

    tops_copy.wait()
    joined_ref[pl.ds(0, share)] = begin_ref[...].astype(BF)
    joined_ref[pl.ds(share, piece)] = tops_ref[...]
    lane = lax.broadcasted_iota(jnp.int32, (share, width), 1)
    sub = lax.broadcasted_iota(jnp.int32, (share, width), 0)
    unit = jnp.where(lane == row * share + sub, 1.0, 0.0).astype(BF)
    stacks_ref[...] = jnp.zeros_like(stacks_ref)
    stacks_ref[0, pl.ds(0, share)] = unit
    stack, at = unit, 0
    for k in range(supers):
        reach_ref[pl.ds(at, (k + 1) * share)] = dot_nt(stack, panel_ref[k]).astype(BF)
        at += (k + 1) * share
        copies[k].wait()
        stack = jnp.concatenate([dot_nt(stack, l_ref[k]).astype(BF), unit], 0)
        stacks_ref[k + 1, pl.ds(0, (k + 2) * share)] = stack


def place(refs, order, write):
    me = lax.axis_index("rows")
    for ref, offset in zip(refs, order):
        write(me ^ offset, ref)


def begin_kernel(n_cols, n_rows, order, l_ref, panel_ref, stacks_ref, *refs):
    got = refs[: len(order)]
    begin_ref, ahead_ref, x_ref, y_ref = refs[len(order) :]
    supers, width, _ = l_ref.shape
    share, piece = width // n_rows, y_ref.shape[0] // n_rows
    col = lax.axis_index("cols")

    def write(at, ref):
        x_ref[pl.ds(pl.multiple_of(at * share, share), share)] = ref[pl.ds(0, share)]
        y_ref[pl.ds(pl.multiple_of(at * piece, piece), piece)] = ref[pl.ds(share, piece)]

    place(got, order, write)
    begin = dot(stacks_ref[jnp.maximum(supers - col, 0)], x_ref[...])
    begin_ref[...] = begin
    first = jnp.where(col == 0, begin, 0.0).astype(BF)
    across = dot_nt(stacks_ref[supers], y_ref[...]).astype(BF)
    ahead_ref[...] = dot(first, l_ref[supers - 1]) + dot(across, panel_ref[supers - 1])


def rows_kernel(n_cols, n_rows, order, levels, last, l_ref, panel_ref, stacks_ref, reach_ref, begin_ref, from_ref, *refs):
    got, refs = refs[: len(order)], refs[len(order) :]
    pieces, refs = refs[:n_cols], refs[n_cols:]
    *acc_refs, y_ref, done_ref = refs
    supers, width, _ = l_ref.shape
    share = width // n_rows
    piece = y_ref.shape[1] // n_rows
    part = share // n_cols
    col = lax.axis_index("cols")
    top = levels[0] == supers - 1

    def write(at, ref):
        for k in range(levels[-1], levels[0] + (1 if top else 2)):
            y_ref[k, pl.ds(pl.multiple_of(at * piece, piece), piece)] = ref[k]

    place(got, order, write)
    acc = from_ref[...]
    for i, k in enumerate(levels):
        here = (k + 1) * share
        if k == supers - 1:
            full = acc
        else:
            across = dot_nt(stacks_ref[k + 1, pl.ds(0, here + share)], y_ref[k + 1]).astype(BF)
            full = dot(acc.astype(BF), l_ref[k]) + dot(across, panel_ref[k])
        acc = full[:here] - dot(reach_ref[pl.ds(sum((j + 1) * share for j in range(k)), here)], y_ref[k])
        done_ref[2 * i] = acc[k * share :].astype(BF)
        done_ref[2 * i + 1] = (-full[here:]).astype(BF)
        if k:
            acc = acc + jnp.where(col == supers - k, begin_ref[pl.ds(0, here)], 0.0)
    if not last:
        acc_refs[0][...] = acc
    for j, out in enumerate(pieces):
        out[...] = done_ref[:, pl.ds(pl.multiple_of((col ^ j) * part, part), part)]


def sum_kernel(own_ref, *refs):
    *got_refs, out_ref = refs
    for i in range(own_ref.shape[0]):
        total = own_ref[i].astype(F32)
        for got in got_refs:
            total = total + got[i].astype(F32)
        out_ref[i] = total.astype(BF)


def last_kernel(n_cols, offsets, levels, diag_ref, *refs):
    got_refs = refs[:n_cols]
    diag_out, sub_out, done_ref, sems = refs[-4:]
    part = got_refs[0].shape[1]
    col = lax.axis_index("cols")
    copies = []
    for i, k in enumerate(levels):
        for j, got in zip(offsets, got_refs):
            rows = pl.ds(pl.multiple_of((col ^ j) * part, part), part)
            done_ref[2 * i, rows] = diag_ref[k, rows] + got[2 * i].astype(F32)
            done_ref[2 * i + 1, rows] = got[2 * i + 1].astype(F32)
        copies.append(fetch(done_ref.at[2 * i], diag_out.at[k], sems.at[2 * i]))
        copies.append(fetch(done_ref.at[2 * i + 1], sub_out.at[k], sems.at[2 * i + 1]))
    for copy in copies:
        copy.wait()


def call(kernel, outs, *args, scratch=(), away=(), out_away=False, aliases=None, flops=0, moved=0):
    vmem, hbm = pl.BlockSpec(memory_space=pltpu.VMEM), pl.BlockSpec(memory_space=pltpu.HBM)
    return pl.pallas_call(
        kernel,
        out_shape=tuple(jax.ShapeDtypeStruct(s, d) for s, d in outs),
        in_specs=[hbm if i in away else vmem for i in range(len(args))],
        out_specs=tuple(hbm if out_away else vmem for _ in outs),
        input_output_aliases=aliases or {},
        scratch_shapes=scratch,
        compiler_params=pltpu.CompilerParams(vmem_limit_bytes=VMEM_BYTES),
        cost_estimate=pl.CostEstimate(flops=flops, bytes_accessed=moved, transcendentals=0),
    )(*[pltpu.with_memory_space_constraint(a, pltpu.HBM) if i in away else a for i, a in enumerate(args)])


def exchange_rows(x):
    near = [x] + [hop(x, "rows", j) for j in ROW_ORDER[1:4]]
    return near + [hop(p, "rows", 1) for p in near]


def local(known_inverse, lower_panel, chain_panel, diag_inverse, top_cols, top_diag, pattern):
    n_rows = lax.axis_size("rows")
    n_cols = lax.axis_size("cols")
    supers = lower_panel.shape[0]
    piece = known_inverse.shape[2]
    width = lower_panel.shape[-1]
    share = width // n_rows
    if n_rows != len(ROW_ORDER) or n_cols != 1 + len(FIRST_ORDER) or n_cols < supers or share % (16 * n_cols) or piece % 16:
        return general(known_inverse, lower_panel, chain_panel, diag_inverse, top_cols, top_diag, pattern)
    known = known_inverse[:, 0]
    tops = top_cols[0, 0]
    block = n_rows * piece
    ways = range(1, n_cols)
    rows_of = [(k + 1) * share for k in range(supers + 1)]
    panel, mask, own, *sent = call(
        functools.partial(first_kernel, n_cols, n_rows),
        [((supers, block, width), BF), ((supers, 8, width), F32)] + [((supers, piece, width), BF)] * n_cols,
        known, lower_panel[:, 0], pattern, away=range(3),
        scratch=[
            pltpu.VMEM((n_cols * piece, block), BF), pltpu.VMEM((supers, n_rows, piece, width), BF),
            pltpu.SMEM(pattern.shape, jnp.int32), pltpu.SemaphoreType.DMA((1 + supers + n_cols,)),
        ],
        flops=2 * known.size * supers * width, moved=4 * block * width * supers,
    )
    got = [hop(sent[j - 1], "cols", j) for j in FIRST_ORDER]
    links, stacks, reach, joined = call(
        functools.partial(ready_kernel, n_cols, n_rows),
        [(chain_panel.shape, BF), ((supers + 1, rows_of[supers], width), BF), ((sum(rows_of[:supers]), block), BF), ((share + piece, width), BF)],
        chain_panel, diag_inverse, top_diag, tops, panel, away=range(4),
        scratch=[pltpu.VMEM((share, width), F32), pltpu.VMEM((piece, width), BF), pltpu.SemaphoreType.DMA((supers + 2,))],
        flops=2 * 12 * share * width * width, moved=4 * width * width * supers,
    )
    begin, ahead = call(
        functools.partial(begin_kernel, n_cols, n_rows, ROW_ORDER),
        [((rows_of[supers], width), F32)] * 2,
        links, panel, stacks, *exchange_rows(joined),
        scratch=[pltpu.VMEM((width, width), BF), pltpu.VMEM((block, width), BF)],
        flops=2 * 15 * share * width * width, moved=4 * width * width,
    )
    cols, cols_out = call(
        chain_kernel,
        [((supers, piece, width), BF)] * 2,
        links, joined, mask, own, *got,
        flops=2 * piece * width * width * supers, moved=2 * width * width * supers,
    )
    arrived = exchange_rows(cols)
    split = supers // 2
    groups = [tuple(reversed(range(split, supers))), tuple(reversed(range(split)))]
    state, parts = ahead, []
    for levels in groups:
        last = levels[-1] == 0
        count = 2 * len(levels)
        *pieces, state = call(
            functools.partial(rows_kernel, n_cols, n_rows, ROW_ORDER, levels, last),
            [((count, share // n_cols, width), BF)] * n_cols + ([] if last else [((levels[-1] * share + share, width), F32)]),
            links, panel, stacks, reach, begin, state, *arrived,
            scratch=[pltpu.VMEM((supers, block, width), BF), pltpu.VMEM((count, share, width), BF)],
            flops=2 * 10 * share * width * width, moved=4 * width * width * supers,
        ) + ((None,) if last else ())
        parts.append((levels, pieces))
    sums = []
    for levels, pieces in parts:
        got = [hop(pieces[j], "cols", j) for j in SUM_ORDER]
        sums.append((levels, call(sum_kernel, [(pieces[0].shape, BF)], pieces[0], *got)[0]))
    filled = ()
    for levels, summed in sums:
        offsets = (0,) + LAST_ORDER
        got = [summed] + [hop(summed, "cols", j) for j in offsets[1:]]
        filled = call(
            functools.partial(last_kernel, n_cols, offsets, levels),
            [(diag_inverse.shape, F32)] * 2,
            diag_inverse, *got, *filled, away=range(1 + n_cols, 1 + n_cols + len(filled)), out_away=True,
            aliases={1 + n_cols + i: i for i in range(len(filled))},
            scratch=[pltpu.VMEM((2 * len(levels), share, width), F32), pltpu.SemaphoreType.DMA((2 * len(levels),))],
        )
    diag, sub = filled
    return cols_out.reshape(supers, 1, 1, piece, width), diag, sub


def solution(mesh):
    in_specs = (
        P(None, "rows", None, "cols"),
        P(None, "cols", None, None, None),
        P(),
        P(None, "rows", None),
        P("cols", "rows", None, None),
        P("rows", None),
        P(),
    )
    out_specs = (P(None, "cols", "rows", None, None), P(None, "rows", None), P(None, "rows", None))
    return jax.shard_map(local, mesh=mesh, in_specs=in_specs, out_specs=out_specs, check_vma=False)
```

```python
import functools

import jax
import jax.numpy as jnp
from jax import lax
from jax.experimental import pallas as pl
from jax.experimental.pallas import tpu as pltpu
from jax.sharding import PartitionSpec as P

BF = jnp.bfloat16
F32 = jnp.float32
ROW_ORDER = (0, 6, 4, 2, 1, 7, 5, 3)
VMEM_BYTES = 32 << 20
FIRST_ORDER = (3, 1, 2)
SUM_ORDER = (3, 2, 1)
LAST_ORDER = (1, 2, 3)


def dot(a, b):
    return jnp.dot(a, b, preferred_element_type=F32)


def dot_nt(a, b):
    return lax.dot_general(a, b, (((1,), (1,)), ((), ())), preferred_element_type=F32)


def pow2(n):
    return n & (n - 1) == 0


def target(i, j, n):
    return i ^ j if pow2(n) else (i + j) % n


def source(i, j, n):
    return i ^ j if pow2(n) else (i - j) % n


def hop(x, axis, j):
    n = lax.axis_size(axis)
    return lax.ppermute(x, axis, [(i, target(i, j, n)) for i in range(n)])


def gather_rows(x):
    n = lax.axis_size("rows")
    me = lax.axis_index("rows")
    if n == 8:
        parts = [x] + [hop(x, "rows", j) for j in (6, 4, 2)]
        offsets = [0, 6, 4, 2]
        here = jnp.stack(parts)
        there = hop(here, "rows", 1)
        whole = jnp.concatenate([here, there], 0)
        offsets = offsets + [o ^ 1 for o in offsets]
        return whole, [source(me, o, n) for o in offsets]
    if pow2(n):
        whole, offsets, bit = x[None], [0], n // 2
        while bit:
            whole = jnp.concatenate([whole, hop(whole, "rows", bit)], 0)
            offsets = offsets + [o ^ bit for o in offsets]
            bit //= 2
        return whole, [source(me, o, n) for o in offsets]
    return lax.all_gather(x, "rows"), list(range(n))


def scatter_cols(pieces):
    n = lax.axis_size("cols")
    me = lax.axis_index("cols")
    total = lax.dynamic_index_in_dim(pieces, me, 0, False).astype(F32)
    for j in reversed(range(1, n)):
        sent = lax.dynamic_index_in_dim(pieces, target(me, j, n), 0, False)
        total = total + hop(sent, "cols", j).astype(F32)
    return total


def gather_cols(x):
    n = lax.axis_size("cols")
    me = lax.axis_index("cols")
    whole = jnp.zeros((n,) + x.shape, x.dtype)
    got = [(me, x)] + [(source(me, j, n), hop(x, "cols", j)) for j in reversed(range(1, n))]
    for at, piece in got:
        whole = lax.dynamic_update_index_in_dim(whole, piece, at, 0)
    return whole


def general(known_inverse, lower_panel, chain_panel, diag_inverse, top_cols, top_diag, pattern):
    n_rows = lax.axis_size("rows")
    n_cols = lax.axis_size("cols")
    row_id = lax.axis_index("rows")
    col_id = lax.axis_index("cols")
    supers = lower_panel.shape[0]
    piece = known_inverse.shape[2]
    width = lower_panel.shape[-1]
    share = width // n_rows
    known = known_inverse.reshape(n_cols * piece, -1)
    group_mask = lax.dynamic_slice_in_dim(pattern, col_id * n_rows, n_rows, 1).astype(BF)
    panels = lower_panel[:, 0] * group_mask[:, :, None, None]
    own_mask = lax.dynamic_index_in_dim(group_mask, row_id, 1, keepdims=False).astype(F32)

    slabs = panels.reshape(supers, n_rows * piece, width)
    partial = jnp.stack([dot(known, slabs[k]).astype(BF).reshape(n_cols, piece, width) for k in range(supers)], 1)
    product = scatter_cols(partial)

    start = [top_diag] + [diag_inverse[k] for k in reversed(range(1, supers))]
    level_of = lambda c: supers - c
    mine = jnp.zeros((share, width), F32)
    for i, s in enumerate(start):
        mine = jnp.where(col_id % len(start) == i, s, mine) if n_cols <= len(start) else jnp.where(col_id == i, s, mine)
    joined = jnp.concatenate([mine.astype(BF), top_cols.reshape(piece, width)], 0)
    gathered, order = gather_rows(joined)
    shares = gathered[:, :share].reshape(width, width)
    tops = gathered[:, share:].reshape(n_rows * piece, width)
    order = jnp.stack([jnp.asarray(o, jnp.int32) for o in order])
    panel_rel = [p[order].reshape(n_rows * piece, width) for p in panels]
    own_rows = (lax.broadcasted_iota(jnp.int32, (share, width), 1) == row_id * share + lax.broadcasted_iota(jnp.int32, (share, width), 0)).astype(BF)
    stacks = [own_rows]
    for k in range(supers):
        stacks.append(jnp.concatenate([dot_nt(stacks[k], chain_panel[k]).astype(BF), own_rows], 0))
    begins = []
    for k in range(supers + 1):
        rel = stacks[k].reshape(-1, n_rows, share)[:, order].reshape(-1, width)
        begins.append(dot(rel, shares))
    reach = [dot_nt(stacks[k], panel_rel[k]).astype(BF) for k in range(supers)]

    prev = top_cols.reshape(piece, width)
    cols_list = [None] * supers
    for k in reversed(range(supers)):
        carried = dot(prev, chain_panel[k])
        prev = (-(product[k] + carried) * own_mask[k]).astype(BF)
        cols_list[k] = prev
    cols_out = jnp.stack(cols_list)
    all_cols, _ = gather_rows(cols_out)
    slab_cols = [all_cols[:, k].reshape(n_rows * piece, width) for k in range(supers)] + [tops]

    acc = jnp.where(col_id == 0, begins[supers], 0.0)
    diag_list = [None] * supers
    sub_list = [None] * supers
    for k in reversed(range(supers)):
        across = dot_nt(stacks[k + 1], slab_cols[k + 1]).astype(BF)
        full = dot(acc.astype(BF), chain_panel[k]) + dot(across, panel_rel[k])
        sub_list[k] = -full[(k + 1) * share:]
        acc = full[: (k + 1) * share] - dot(reach[k], slab_cols[k])
        diag_list[k] = acc[k * share :]
        if k:
            acc = acc + jnp.where(col_id == level_of(k), begins[k], 0.0)
    done = jnp.stack(diag_list + sub_list)
    if share % n_cols == 0:
        part = share // n_cols
        pieces = jnp.swapaxes(done.astype(BF).reshape(2 * supers, n_cols, part, width), 0, 1)
        summed = gather_cols(scatter_cols(pieces).astype(BF))
        summed = jnp.swapaxes(summed, 0, 1).reshape(2 * supers, share, width)
    else:
        summed = lax.psum(done.astype(BF), "cols")
    summed = summed.astype(F32)
    return (
        cols_out.reshape(supers, 1, 1, piece, width),
        diag_inverse + summed[:supers],
        summed[supers:],
    )


def fetch(source, into, sem):
    copy = pltpu.make_async_copy(source, into, sem)
    copy.start()
    return copy


def first_kernel(n_cols, n_rows, g_any, m_any, pattern_any, *refs):
    panel_ref, mask_ref = refs[:2]
    piece_refs = refs[2 : 2 + n_cols]
    g_ref, order_ref, m_ref, pattern_ref, sems = refs[2 + n_cols :]
    col, row = lax.axis_index("cols"), lax.axis_index("rows")
    supers, _, piece, _ = m_ref.shape
    pattern_copy = fetch(pattern_any, pattern_ref, sems.at[0])
    panel_copy = fetch(m_any, m_ref, sems.at[1])
    g_copy = fetch(g_any, g_ref, sems.at[2])
    g_copy.wait()
    for j in range(n_cols):
        order_ref[pl.ds(j * piece, piece)] = g_ref[col ^ j]
    pattern_copy.wait()
    panel_copy.wait()
    for k in range(supers):
        mask_ref[k] = jnp.full(mask_ref.shape[1:], pattern_ref[k, col * n_rows + row].astype(F32))
        for r in range(n_rows):
            on = pattern_ref[k, col * n_rows + r] != 0
            panel_ref[k, pl.ds(r * piece, piece)] = jnp.where(on, m_ref[k, r], jnp.zeros_like(m_ref[k, r]))
        product = dot(order_ref[...], panel_ref[k]).astype(BF)
        for j, out in enumerate(piece_refs):
            out[k] = product[j * piece : (j + 1) * piece]


def chain_kernel(l_ref, carry_ref, mask_ref, own_ref, *refs):
    *got_refs, cols_ref, copy_ref = refs
    supers, piece, _ = own_ref.shape
    carried = carry_ref[...]
    for k in reversed(range(supers)):
        total = own_ref[k].astype(F32)
        for got in got_refs:
            total = total + got[k].astype(F32)
        total = total + (carried if k == supers - 1 else dot(prev, l_ref[k]))
        prev = (-(total * mask_ref[k, pl.ds(0, 1)])).astype(BF)
        cols_ref[k] = prev
        copy_ref[k] = prev


def place(refs, order, write):
    me = lax.axis_index("rows")
    for ref, offset in zip(refs, order):
        write(me ^ offset, ref)


def ready_kernel(n_cols, n_rows, l_any, diag_any, top_any, tops_any, panel_ref, *refs):
    l_ref, stacks_ref, reach_ref, joined_ref, carry_ref, begin_ref, tops_ref, sems = refs
    supers, width, _ = l_ref.shape
    share, piece = width // n_rows, tops_ref.shape[0]
    col, row = lax.axis_index("cols"), lax.axis_index("rows")
    copies = [fetch(l_any.at[k], l_ref.at[k], sems.at[k]) for k in range(supers)]
    tops_copy = fetch(tops_any, tops_ref, sems.at[supers])

    @pl.when(col == 0)
    def _():
        fetch(top_any, begin_ref, sems.at[supers + 1]).wait()

    @pl.when(jnp.logical_and(col > 0, col < supers))
    def _():
        fetch(diag_any.at[jnp.clip(supers - col, 1, supers - 1)], begin_ref, sems.at[supers + 1]).wait()

    @pl.when(col >= supers)
    def _():
        begin_ref[...] = jnp.zeros_like(begin_ref)

    tops_copy.wait()
    joined_ref[pl.ds(0, share)] = begin_ref[...].astype(BF)
    joined_ref[pl.ds(share, piece)] = tops_ref[...]
    lane = lax.broadcasted_iota(jnp.int32, (share, width), 1)
    sub = lax.broadcasted_iota(jnp.int32, (share, width), 0)
    unit = jnp.where(lane == row * share + sub, 1.0, 0.0).astype(BF)
    stacks_ref[...] = jnp.zeros_like(stacks_ref)
    stacks_ref[0, pl.ds(0, share)] = unit
    stack, at = unit, 0
    for k in range(supers):
        reach_ref[pl.ds(at, (k + 1) * share)] = dot_nt(stack, panel_ref[k]).astype(BF)
        at += (k + 1) * share
        copies[k].wait()
        stack = jnp.concatenate([dot_nt(stack, l_ref[k]).astype(BF), unit], 0)
        stacks_ref[k + 1, pl.ds(0, (k + 2) * share)] = stack
    carry_ref[...] = dot(tops_ref[...], l_ref[supers - 1])


def place(refs, order, write):
    me = lax.axis_index("rows")
    for ref, offset in zip(refs, order):
        write(me ^ offset, ref)


def begin_kernel(n_cols, n_rows, order, l_ref, panel_ref, stacks_ref, *refs):
    got = refs[: len(order)]
    begin_ref, ahead_ref, x_ref, y_ref = refs[len(order) :]
    supers, width, _ = l_ref.shape
    share, piece = width // n_rows, y_ref.shape[0] // n_rows
    col = lax.axis_index("cols")

    def write(at, ref):
        x_ref[pl.ds(pl.multiple_of(at * share, share), share)] = ref[pl.ds(0, share)]
        y_ref[pl.ds(pl.multiple_of(at * piece, piece), piece)] = ref[pl.ds(share, piece)]

    place(got, order, write)
    begin = dot(stacks_ref[jnp.maximum(supers - col, 0)], x_ref[...])
    begin_ref[...] = begin
    first = jnp.where(col == 0, begin, 0.0).astype(BF)
    across = dot_nt(stacks_ref[supers], y_ref[...]).astype(BF)
    ahead_ref[...] = dot(first, l_ref[supers - 1]) + dot(across, panel_ref[supers - 1])


def rows_kernel(n_cols, n_rows, order, levels, last, l_ref, panel_ref, stacks_ref, reach_ref, begin_ref, from_ref, *refs):
    got, refs = refs[: len(order)], refs[len(order) :]
    pieces, refs = refs[:n_cols], refs[n_cols:]
    *acc_refs, y_ref, done_ref = refs
    supers, width, _ = l_ref.shape
    share = width // n_rows
    piece = y_ref.shape[1] // n_rows
    part = share // n_cols
    col = lax.axis_index("cols")
    top = levels[0] == supers - 1

    def write(at, ref):
        for k in range(levels[-1], levels[0] + (1 if top else 2)):
            y_ref[k, pl.ds(pl.multiple_of(at * piece, piece), piece)] = ref[k]

    place(got, order, write)
    acc = from_ref[...]
    for i, k in enumerate(levels):
        here = (k + 1) * share
        if k == supers - 1:
            full = acc
        else:
            across = dot_nt(stacks_ref[k + 1, pl.ds(0, here + share)], y_ref[k + 1]).astype(BF)
            full = dot(acc.astype(BF), l_ref[k]) + dot(across, panel_ref[k])
        acc = full[:here] - dot(reach_ref[pl.ds(sum((j + 1) * share for j in range(k)), here)], y_ref[k])
        done_ref[2 * i] = acc[k * share :].astype(BF)
        done_ref[2 * i + 1] = (-full[here:]).astype(BF)
        if k:
            acc = acc + jnp.where(col == supers - k, begin_ref[pl.ds(0, here)], 0.0)
    if not last:
        acc_refs[0][...] = acc
    for j, out in enumerate(pieces):
        out[...] = done_ref[:, pl.ds(pl.multiple_of((col ^ j) * part, part), part)]


def sum_kernel(own_ref, *refs):
    *got_refs, out_ref = refs
    for i in range(own_ref.shape[0]):
        total = own_ref[i].astype(F32)
        for got in got_refs:
            total = total + got[i].astype(F32)
        out_ref[i] = total.astype(BF)


def last_kernel(n_cols, offsets, levels, diag_ref, *refs):
    got_refs = refs[:n_cols]
    diag_out, sub_out, done_ref, sems = refs[-4:]
    part = got_refs[0].shape[1]
    col = lax.axis_index("cols")
    copies = []
    for i, k in enumerate(levels):
        for j, got in zip(offsets, got_refs):
            rows = pl.ds(pl.multiple_of((col ^ j) * part, part), part)
            done_ref[2 * i, rows] = diag_ref[k, rows] + got[2 * i].astype(F32)
            done_ref[2 * i + 1, rows] = got[2 * i + 1].astype(F32)
        copies.append(fetch(done_ref.at[2 * i], diag_out.at[k], sems.at[2 * i]))
        copies.append(fetch(done_ref.at[2 * i + 1], sub_out.at[k], sems.at[2 * i + 1]))
    for copy in copies:
        copy.wait()


def call(kernel, outs, *args, scratch=(), away=(), out_away=False, aliases=None, flops=0, moved=0):
    vmem, hbm = pl.BlockSpec(memory_space=pltpu.VMEM), pl.BlockSpec(memory_space=pltpu.HBM)
    return pl.pallas_call(
        kernel,
        out_shape=tuple(jax.ShapeDtypeStruct(s, d) for s, d in outs),
        in_specs=[hbm if i in away else vmem for i in range(len(args))],
        out_specs=tuple(hbm if out_away else vmem for _ in outs),
        input_output_aliases=aliases or {},
        scratch_shapes=scratch,
        compiler_params=pltpu.CompilerParams(vmem_limit_bytes=VMEM_BYTES),
        cost_estimate=pl.CostEstimate(flops=flops, bytes_accessed=moved, transcendentals=0),
    )(*[pltpu.with_memory_space_constraint(a, pltpu.HBM) if i in away else a for i, a in enumerate(args)])


def exchange_rows(x):
    near = [x] + [hop(x, "rows", j) for j in ROW_ORDER[1:4]]
    return near + [hop(p, "rows", 1) for p in near]


def local(known_inverse, lower_panel, chain_panel, diag_inverse, top_cols, top_diag, pattern):
    n_rows = lax.axis_size("rows")
    n_cols = lax.axis_size("cols")
    supers = lower_panel.shape[0]
    piece = known_inverse.shape[2]
    width = lower_panel.shape[-1]
    share = width // n_rows
    if n_rows != len(ROW_ORDER) or n_cols != 1 + len(FIRST_ORDER) or n_cols < supers or share % (16 * n_cols) or piece % 16:
        return general(known_inverse, lower_panel, chain_panel, diag_inverse, top_cols, top_diag, pattern)
    known = known_inverse[:, 0]
    tops = top_cols[0, 0]
    block = n_rows * piece
    ways = range(1, n_cols)
    rows_of = [(k + 1) * share for k in range(supers + 1)]
    panel, mask, own, *sent = call(
        functools.partial(first_kernel, n_cols, n_rows),
        [((supers, block, width), BF), ((supers, 8, width), F32)] + [((supers, piece, width), BF)] * n_cols,
        known, lower_panel[:, 0], pattern, away=range(3),
        scratch=[
            pltpu.VMEM(known.shape, BF), pltpu.VMEM((n_cols * piece, block), BF), pltpu.VMEM((supers, n_rows, piece, width), BF),
            pltpu.SMEM(pattern.shape, jnp.int32), pltpu.SemaphoreType.DMA((3,)),
        ],
        flops=2 * known.size * supers * width, moved=4 * block * width * supers,
    )
    got = [hop(sent[j - 1], "cols", j) for j in FIRST_ORDER]
    links, stacks, reach, joined, carry = call(
        functools.partial(ready_kernel, n_cols, n_rows),
        [(chain_panel.shape, BF), ((supers + 1, rows_of[supers], width), BF), ((sum(rows_of[:supers]), block), BF), ((share + piece, width), BF), ((piece, width), F32)],
        chain_panel, diag_inverse, top_diag, tops, panel, away=range(4),
        scratch=[pltpu.VMEM((share, width), F32), pltpu.VMEM((piece, width), BF), pltpu.SemaphoreType.DMA((supers + 2,))],
        flops=2 * 12 * share * width * width, moved=4 * width * width * supers,
    )
    begin, ahead = call(
        functools.partial(begin_kernel, n_cols, n_rows, ROW_ORDER),
        [((rows_of[supers], width), F32)] * 2,
        links, panel, stacks, *exchange_rows(joined),
        scratch=[pltpu.VMEM((width, width), BF), pltpu.VMEM((block, width), BF)],
        flops=2 * 15 * share * width * width, moved=4 * width * width,
    )
    cols, cols_out = call(
        chain_kernel,
        [((supers, piece, width), BF)] * 2,
        links, carry, mask, own, *got,
        flops=2 * piece * width * width * supers, moved=2 * width * width * supers,
    )
    arrived = exchange_rows(cols)
    split = supers // 2
    groups = [tuple(reversed(range(split, supers))), tuple(reversed(range(split)))]
    state, parts = ahead, []
    for levels in groups:
        last = levels[-1] == 0
        count = 2 * len(levels)
        *pieces, state = call(
            functools.partial(rows_kernel, n_cols, n_rows, ROW_ORDER, levels, last),
            [((count, share // n_cols, width), BF)] * n_cols + ([] if last else [((levels[-1] * share + share, width), F32)]),
            links, panel, stacks, reach, begin, state, *arrived,
            scratch=[pltpu.VMEM((supers, block, width), BF), pltpu.VMEM((count, share, width), BF)],
            flops=2 * 10 * share * width * width, moved=4 * width * width * supers,
        ) + ((None,) if last else ())
        parts.append((levels, pieces))
    sums = []
    for levels, pieces in parts:
        got = [hop(pieces[j], "cols", j) for j in SUM_ORDER]
        sums.append((levels, call(sum_kernel, [(pieces[0].shape, BF)], pieces[0], *got)[0]))
    filled = ()
    for levels, summed in sums:
        offsets = (0,) + LAST_ORDER
        got = [summed] + [hop(summed, "cols", j) for j in offsets[1:]]
        filled = call(
            functools.partial(last_kernel, n_cols, offsets, levels),
            [(diag_inverse.shape, F32)] * 2,
            diag_inverse, *got, *filled, away=range(1 + n_cols, 1 + n_cols + len(filled)), out_away=True,
            aliases={1 + n_cols + i: i for i in range(len(filled))},
            scratch=[pltpu.VMEM((2 * len(levels), share, width), F32), pltpu.SemaphoreType.DMA((2 * len(levels),))],
        )
    diag, sub = filled
    return cols_out.reshape(supers, 1, 1, piece, width), diag, sub


def solution(mesh):
    in_specs = (
        P(None, "rows", None, "cols"),
        P(None, "cols", None, None, None),
        P(),
        P(None, "rows", None),
        P("cols", "rows", None, None),
        P("rows", None),
        P(),
    )
    out_specs = (P(None, "cols", "rows", None, None), P(None, "rows", None), P(None, "rows", None))
    return jax.shard_map(local, mesh=mesh, in_specs=in_specs, out_specs=out_specs, check_vma=False)
```

```python
import functools

import jax
import jax.numpy as jnp
from jax import lax
from jax.experimental import pallas as pl
from jax.experimental.pallas import tpu as pltpu
from jax.sharding import PartitionSpec as P

BF = jnp.bfloat16
F32 = jnp.float32
ROW_ORDER = (0, 6, 4, 2, 1, 7, 5, 3)
VMEM_BYTES = 32 << 20
FIRST_ORDER = (3, 1, 2)
SUM_ORDER = (3, 2, 1)
LAST_ORDER = (1, 2, 3)


def dot(a, b):
    return jnp.dot(a, b, preferred_element_type=F32)


def dot_nt(a, b):
    return lax.dot_general(a, b, (((1,), (1,)), ((), ())), preferred_element_type=F32)


def pow2(n):
    return n & (n - 1) == 0


def target(i, j, n):
    return i ^ j if pow2(n) else (i + j) % n


def source(i, j, n):
    return i ^ j if pow2(n) else (i - j) % n


def hop(x, axis, j):
    n = lax.axis_size(axis)
    return lax.ppermute(x, axis, [(i, target(i, j, n)) for i in range(n)])


def gather_rows(x):
    n = lax.axis_size("rows")
    me = lax.axis_index("rows")
    if n == 8:
        parts = [x] + [hop(x, "rows", j) for j in (6, 4, 2)]
        offsets = [0, 6, 4, 2]
        here = jnp.stack(parts)
        there = hop(here, "rows", 1)
        whole = jnp.concatenate([here, there], 0)
        offsets = offsets + [o ^ 1 for o in offsets]
        return whole, [source(me, o, n) for o in offsets]
    if pow2(n):
        whole, offsets, bit = x[None], [0], n // 2
        while bit:
            whole = jnp.concatenate([whole, hop(whole, "rows", bit)], 0)
            offsets = offsets + [o ^ bit for o in offsets]
            bit //= 2
        return whole, [source(me, o, n) for o in offsets]
    return lax.all_gather(x, "rows"), list(range(n))


def scatter_cols(pieces):
    n = lax.axis_size("cols")
    me = lax.axis_index("cols")
    total = lax.dynamic_index_in_dim(pieces, me, 0, False).astype(F32)
    for j in reversed(range(1, n)):
        sent = lax.dynamic_index_in_dim(pieces, target(me, j, n), 0, False)
        total = total + hop(sent, "cols", j).astype(F32)
    return total


def gather_cols(x):
    n = lax.axis_size("cols")
    me = lax.axis_index("cols")
    whole = jnp.zeros((n,) + x.shape, x.dtype)
    got = [(me, x)] + [(source(me, j, n), hop(x, "cols", j)) for j in reversed(range(1, n))]
    for at, piece in got:
        whole = lax.dynamic_update_index_in_dim(whole, piece, at, 0)
    return whole


def general(known_inverse, lower_panel, chain_panel, diag_inverse, top_cols, top_diag, pattern):
    n_rows = lax.axis_size("rows")
    n_cols = lax.axis_size("cols")
    row_id = lax.axis_index("rows")
    col_id = lax.axis_index("cols")
    supers = lower_panel.shape[0]
    piece = known_inverse.shape[2]
    width = lower_panel.shape[-1]
    share = width // n_rows
    known = known_inverse.reshape(n_cols * piece, -1)
    group_mask = lax.dynamic_slice_in_dim(pattern, col_id * n_rows, n_rows, 1).astype(BF)
    panels = lower_panel[:, 0] * group_mask[:, :, None, None]
    own_mask = lax.dynamic_index_in_dim(group_mask, row_id, 1, keepdims=False).astype(F32)

    slabs = panels.reshape(supers, n_rows * piece, width)
    partial = jnp.stack([dot(known, slabs[k]).astype(BF).reshape(n_cols, piece, width) for k in range(supers)], 1)
    product = scatter_cols(partial)

    start = [top_diag] + [diag_inverse[k] for k in reversed(range(1, supers))]
    level_of = lambda c: supers - c
    mine = jnp.zeros((share, width), F32)
    for i, s in enumerate(start):
        mine = jnp.where(col_id % len(start) == i, s, mine) if n_cols <= len(start) else jnp.where(col_id == i, s, mine)
    joined = jnp.concatenate([mine.astype(BF), top_cols.reshape(piece, width)], 0)
    gathered, order = gather_rows(joined)
    shares = gathered[:, :share].reshape(width, width)
    tops = gathered[:, share:].reshape(n_rows * piece, width)
    order = jnp.stack([jnp.asarray(o, jnp.int32) for o in order])
    panel_rel = [p[order].reshape(n_rows * piece, width) for p in panels]
    own_rows = (lax.broadcasted_iota(jnp.int32, (share, width), 1) == row_id * share + lax.broadcasted_iota(jnp.int32, (share, width), 0)).astype(BF)
    stacks = [own_rows]
    for k in range(supers):
        stacks.append(jnp.concatenate([dot_nt(stacks[k], chain_panel[k]).astype(BF), own_rows], 0))
    begins = []
    for k in range(supers + 1):
        rel = stacks[k].reshape(-1, n_rows, share)[:, order].reshape(-1, width)
        begins.append(dot(rel, shares))
    reach = [dot_nt(stacks[k], panel_rel[k]).astype(BF) for k in range(supers)]

    prev = top_cols.reshape(piece, width)
    cols_list = [None] * supers
    for k in reversed(range(supers)):
        carried = dot(prev, chain_panel[k])
        prev = (-(product[k] + carried) * own_mask[k]).astype(BF)
        cols_list[k] = prev
    cols_out = jnp.stack(cols_list)
    all_cols, _ = gather_rows(cols_out)
    slab_cols = [all_cols[:, k].reshape(n_rows * piece, width) for k in range(supers)] + [tops]

    acc = jnp.where(col_id == 0, begins[supers], 0.0)
    diag_list = [None] * supers
    sub_list = [None] * supers
    for k in reversed(range(supers)):
        across = dot_nt(stacks[k + 1], slab_cols[k + 1]).astype(BF)
        full = dot(acc.astype(BF), chain_panel[k]) + dot(across, panel_rel[k])
        sub_list[k] = -full[(k + 1) * share:]
        acc = full[: (k + 1) * share] - dot(reach[k], slab_cols[k])
        diag_list[k] = acc[k * share :]
        if k:
            acc = acc + jnp.where(col_id == level_of(k), begins[k], 0.0)
    done = jnp.stack(diag_list + sub_list)
    if share % n_cols == 0:
        part = share // n_cols
        pieces = jnp.swapaxes(done.astype(BF).reshape(2 * supers, n_cols, part, width), 0, 1)
        summed = gather_cols(scatter_cols(pieces).astype(BF))
        summed = jnp.swapaxes(summed, 0, 1).reshape(2 * supers, share, width)
    else:
        summed = lax.psum(done.astype(BF), "cols")
    summed = summed.astype(F32)
    return (
        cols_out.reshape(supers, 1, 1, piece, width),
        diag_inverse + summed[:supers],
        summed[supers:],
    )


def fetch(source, into, sem):
    copy = pltpu.make_async_copy(source, into, sem)
    copy.start()
    return copy


def first_kernel(n_cols, n_rows, g_any, m_any, pattern_any, *refs):
    panel_ref, mask_ref = refs[:2]
    piece_refs = refs[2 : 2 + n_cols]
    g_ref, order_ref, m_ref, pattern_ref, sems = refs[2 + n_cols :]
    col, row = lax.axis_index("cols"), lax.axis_index("rows")
    supers, _, piece, _ = m_ref.shape
    pattern_copy = fetch(pattern_any, pattern_ref, sems.at[0])
    panel_copy = fetch(m_any, m_ref, sems.at[1])
    g_copy = fetch(g_any, g_ref, sems.at[2])
    g_copy.wait()
    for j in range(n_cols):
        order_ref[pl.ds(j * piece, piece)] = g_ref[col ^ j]
    pattern_copy.wait()
    panel_copy.wait()
    for k in range(supers):
        mask_ref[k] = jnp.full(mask_ref.shape[1:], pattern_ref[k, col * n_rows + row].astype(F32))
        for r in range(n_rows):
            on = pattern_ref[k, col * n_rows + r] != 0
            panel_ref[k, pl.ds(r * piece, piece)] = jnp.where(on, m_ref[k, r], jnp.zeros_like(m_ref[k, r]))
        product = dot(order_ref[...], panel_ref[k]).astype(BF)
        for j, out in enumerate(piece_refs):
            out[k] = product[j * piece : (j + 1) * piece]


def chain_kernel(l_ref, carry_ref, mask_ref, own_ref, *refs):
    *got_refs, cols_ref, copy_ref = refs
    supers, piece, _ = own_ref.shape
    carried = carry_ref[...]
    for k in reversed(range(supers)):
        total = own_ref[k].astype(F32)
        for got in got_refs:
            total = total + got[k].astype(F32)
        total = total + (carried if k == supers - 1 else dot(prev, l_ref[k]))
        prev = (-(total * mask_ref[k, pl.ds(0, 1)])).astype(BF)
        cols_ref[k] = prev
        copy_ref[k] = prev


def place(refs, order, write):
    me = lax.axis_index("rows")
    for ref, offset in zip(refs, order):
        write(me ^ offset, ref)


def ready_kernel(n_cols, n_rows, l_any, diag_any, top_any, tops_any, panel_ref, *refs):
    l_ref, stacks_ref, reach_ref, joined_ref, carry_ref, begin_ref, tops_ref, sems = refs
    supers, width, _ = l_ref.shape
    share, piece = width // n_rows, tops_ref.shape[0]
    col, row = lax.axis_index("cols"), lax.axis_index("rows")
    copies = [fetch(l_any.at[0], l_ref.at[0], sems.at[0]), fetch(l_any.at[pl.ds(1, supers - 1)], l_ref.at[pl.ds(1, supers - 1)], sems.at[1])]
    tops_copy = fetch(tops_any, tops_ref, sems.at[supers])

    @pl.when(col == 0)
    def _():
        fetch(top_any, begin_ref, sems.at[supers + 1])

    @pl.when(jnp.logical_and(col > 0, col < supers))
    def _():
        fetch(diag_any.at[jnp.clip(supers - col, 1, supers - 1)], begin_ref, sems.at[supers + 1])

    @pl.when(col >= supers)
    def _():
        begin_ref[...] = jnp.zeros_like(begin_ref)

    lane = lax.broadcasted_iota(jnp.int32, (share, width), 1)
    sub = lax.broadcasted_iota(jnp.int32, (share, width), 0)
    unit = jnp.where(lane == row * share + sub, 1.0, 0.0).astype(BF)
    stacks_ref[...] = jnp.zeros_like(stacks_ref)
    stacks_ref[0, pl.ds(0, share)] = unit
    stack, at = unit, 0
    for k in range(supers):
        reach_ref[pl.ds(at, (k + 1) * share)] = dot_nt(stack, panel_ref[k]).astype(BF)
        at += (k + 1) * share
        if k < 2:
            copies[k].wait()
        stack = jnp.concatenate([dot_nt(stack, l_ref[k]).astype(BF), unit], 0)
        stacks_ref[k + 1, pl.ds(0, (k + 2) * share)] = stack
    tops_copy.wait()
    carry_ref[...] = dot(tops_ref[...], l_ref[supers - 1])

    @pl.when(col < supers)
    def _():
        pltpu.make_async_copy(top_any, begin_ref, sems.at[supers + 1]).wait()

    joined_ref[pl.ds(0, share)] = begin_ref[...].astype(BF)
    joined_ref[pl.ds(share, piece)] = tops_ref[...]


def place(refs, order, write):
    me = lax.axis_index("rows")
    for ref, offset in zip(refs, order):
        write(me ^ offset, ref)


def begin_kernel(n_cols, n_rows, order, l_ref, panel_ref, stacks_ref, *refs):
    got = refs[: len(order)]
    begin_ref, ahead_ref, x_ref, y_ref = refs[len(order) :]
    supers, width, _ = l_ref.shape
    share, piece = width // n_rows, y_ref.shape[0] // n_rows
    col = lax.axis_index("cols")

    def write(at, ref):
        x_ref[pl.ds(pl.multiple_of(at * share, share), share)] = ref[pl.ds(0, share)]
        y_ref[pl.ds(pl.multiple_of(at * piece, piece), piece)] = ref[pl.ds(share, piece)]

    place(got, order, write)
    begin = dot(stacks_ref[jnp.maximum(supers - col, 0)], x_ref[...])
    begin_ref[...] = begin
    across = dot_nt(stacks_ref[supers], y_ref[...]).astype(BF)
    ahead_ref[...] = dot(across, panel_ref[supers - 1])

    @pl.when(col == 0)
    def _():
        ahead_ref[...] += dot(begin.astype(BF), l_ref[supers - 1])


def rows_kernel(n_cols, n_rows, order, levels, last, l_ref, panel_ref, stacks_ref, reach_ref, begin_ref, from_ref, *refs):
    got, refs = refs[: len(order)], refs[len(order) :]
    pieces, refs = refs[:n_cols], refs[n_cols:]
    *acc_refs, y_ref, done_ref = refs
    supers, width, _ = l_ref.shape
    share = width // n_rows
    piece = y_ref.shape[1] // n_rows
    part = share // n_cols
    col = lax.axis_index("cols")
    top = levels[0] == supers - 1

    def write(at, ref):
        for k in range(levels[-1], levels[0] + (1 if top else 2)):
            y_ref[k, pl.ds(pl.multiple_of(at * piece, piece), piece)] = ref[k]

    place(got, order, write)
    acc = from_ref[...]
    for i, k in enumerate(levels):
        here = (k + 1) * share
        if k == supers - 1:
            full = acc
        else:
            across = dot_nt(stacks_ref[k + 1, pl.ds(0, here + share)], y_ref[k + 1]).astype(BF)
            full = dot(acc.astype(BF), l_ref[k]) + dot(across, panel_ref[k])
        acc = full[:here] - dot(reach_ref[pl.ds(sum((j + 1) * share for j in range(k)), here)], y_ref[k])
        done_ref[2 * i] = acc[k * share :].astype(BF)
        done_ref[2 * i + 1] = (-full[here:]).astype(BF)
        if k:
            acc = acc + jnp.where(col == supers - k, begin_ref[pl.ds(0, here)], 0.0)
    if not last:
        acc_refs[0][...] = acc
    for j, out in enumerate(pieces):
        out[...] = done_ref[:, pl.ds(pl.multiple_of((col ^ j) * part, part), part)]


def sum_kernel(own_ref, *refs):
    *got_refs, out_ref = refs
    for i in range(own_ref.shape[0]):
        total = own_ref[i].astype(F32)
        for got in got_refs:
            total = total + got[i].astype(F32)
        out_ref[i] = total.astype(BF)


def last_kernel(n_cols, offsets, levels, diag_ref, *refs):
    got_refs = refs[:n_cols]
    diag_out, sub_out, done_ref, sub_ref, sems = refs[-5:]
    part = got_refs[0].shape[1]
    col = lax.axis_index("cols")
    span = pl.ds(levels[-1], len(levels))
    places = [pl.ds(pl.multiple_of((col ^ j) * part, part), part) for j in offsets]
    for i, k in enumerate(levels):
        for rows, got in zip(places, got_refs):
            sub_ref[k - levels[-1], rows] = got[2 * i + 1].astype(F32)
    sub_copy = fetch(sub_ref, sub_out.at[span], sems.at[0])
    for i, k in enumerate(levels):
        for rows, got in zip(places, got_refs):
            done_ref[k - levels[-1], rows] = diag_ref[k, rows] + got[2 * i].astype(F32)
    diag_copy = fetch(done_ref, diag_out.at[span], sems.at[1])
    sub_copy.wait()
    diag_copy.wait()


def call(kernel, outs, *args, scratch=(), away=(), out_away=False, aliases=None, flops=0, moved=0):
    vmem, hbm = pl.BlockSpec(memory_space=pltpu.VMEM), pl.BlockSpec(memory_space=pltpu.HBM)
    return pl.pallas_call(
        kernel,
        out_shape=tuple(jax.ShapeDtypeStruct(s, d) for s, d in outs),
        in_specs=[hbm if i in away else vmem for i in range(len(args))],
        out_specs=tuple(hbm if out_away else vmem for _ in outs),
        input_output_aliases=aliases or {},
        scratch_shapes=scratch,
        compiler_params=pltpu.CompilerParams(vmem_limit_bytes=VMEM_BYTES),
        cost_estimate=pl.CostEstimate(flops=flops, bytes_accessed=moved, transcendentals=0),
    )(*[pltpu.with_memory_space_constraint(a, pltpu.HBM) if i in away else a for i, a in enumerate(args)])


def exchange_rows(x):
    near = [x] + [hop(x, "rows", j) for j in ROW_ORDER[1:4]]
    return near + [hop(p, "rows", 1) for p in near]


def local(known_inverse, lower_panel, chain_panel, diag_inverse, top_cols, top_diag, pattern):
    n_rows = lax.axis_size("rows")
    n_cols = lax.axis_size("cols")
    supers = lower_panel.shape[0]
    piece = known_inverse.shape[2]
    width = lower_panel.shape[-1]
    share = width // n_rows
    if n_rows != len(ROW_ORDER) or n_cols != 1 + len(FIRST_ORDER) or n_cols < supers or share % (16 * n_cols) or piece % 16:
        return general(known_inverse, lower_panel, chain_panel, diag_inverse, top_cols, top_diag, pattern)
    known = known_inverse[:, 0]
    tops = top_cols[0, 0]
    block = n_rows * piece
    ways = range(1, n_cols)
    rows_of = [(k + 1) * share for k in range(supers + 1)]
    panel, mask, own, *sent = call(
        functools.partial(first_kernel, n_cols, n_rows),
        [((supers, block, width), BF), ((supers, 8, width), F32)] + [((supers, piece, width), BF)] * n_cols,
        known, lower_panel[:, 0], pattern, away=range(3),
        scratch=[
            pltpu.VMEM(known.shape, BF), pltpu.VMEM((n_cols * piece, block), BF), pltpu.VMEM((supers, n_rows, piece, width), BF),
            pltpu.SMEM(pattern.shape, jnp.int32), pltpu.SemaphoreType.DMA((3,)),
        ],
        flops=2 * known.size * supers * width, moved=4 * block * width * supers,
    )
    got = [hop(sent[j - 1], "cols", j) for j in FIRST_ORDER]
    links, stacks, reach, joined, carry = call(
        functools.partial(ready_kernel, n_cols, n_rows),
        [(chain_panel.shape, BF), ((supers + 1, rows_of[supers], width), BF), ((sum(rows_of[:supers]), block), BF), ((share + piece, width), BF), ((piece, width), F32)],
        chain_panel, diag_inverse, top_diag, tops, panel, away=range(4),
        scratch=[pltpu.VMEM((share, width), F32), pltpu.VMEM((piece, width), BF), pltpu.SemaphoreType.DMA((supers + 2,))],
        flops=2 * 12 * share * width * width, moved=4 * width * width * supers,
    )
    begin, ahead = call(
        functools.partial(begin_kernel, n_cols, n_rows, ROW_ORDER),
        [((rows_of[supers], width), F32)] * 2,
        links, panel, stacks, *exchange_rows(joined),
        scratch=[pltpu.VMEM((width, width), BF), pltpu.VMEM((block, width), BF)],
        flops=2 * 15 * share * width * width, moved=4 * width * width,
    )
    cols, cols_out = call(
        chain_kernel,
        [((supers, piece, width), BF)] * 2,
        links, carry, mask, own, *got,
        flops=2 * piece * width * width * supers, moved=2 * width * width * supers,
    )
    arrived = exchange_rows(cols)
    split = supers // 2
    groups = [tuple(reversed(range(split, supers))), tuple(reversed(range(split)))]
    state, parts = ahead, []
    for levels in groups:
        last = levels[-1] == 0
        count = 2 * len(levels)
        *pieces, state = call(
            functools.partial(rows_kernel, n_cols, n_rows, ROW_ORDER, levels, last),
            [((count, share // n_cols, width), BF)] * n_cols + ([] if last else [((levels[-1] * share + share, width), F32)]),
            links, panel, stacks, reach, begin, state, *arrived,
            scratch=[pltpu.VMEM((supers, block, width), BF), pltpu.VMEM((count, share, width), BF)],
            flops=2 * 10 * share * width * width, moved=4 * width * width * supers,
        ) + ((None,) if last else ())
        parts.append((levels, pieces))
    sums = []
    for levels, pieces in parts:
        got = [hop(pieces[j], "cols", j) for j in SUM_ORDER]
        sums.append((levels, call(sum_kernel, [(pieces[0].shape, BF)], pieces[0], *got)[0]))
    filled = ()
    for levels, summed in sums:
        offsets = (0,) + LAST_ORDER
        got = [summed] + [hop(summed, "cols", j) for j in offsets[1:]]
        filled = call(
            functools.partial(last_kernel, n_cols, offsets, levels),
            [(diag_inverse.shape, F32)] * 2,
            diag_inverse, *got, *filled, away=range(1 + n_cols, 1 + n_cols + len(filled)), out_away=True,
            aliases={1 + n_cols + i: i for i in range(len(filled))},
            scratch=[pltpu.VMEM((len(levels), share, width), F32)] * 2 + [pltpu.SemaphoreType.DMA((2,))],
        )
    diag, sub = filled
    return cols_out.reshape(supers, 1, 1, piece, width), diag, sub


def solution(mesh):
    in_specs = (
        P(None, "rows", None, "cols"),
        P(None, "cols", None, None, None),
        P(),
        P(None, "rows", None),
        P("cols", "rows", None, None),
        P("rows", None),
        P(),
    )
    out_specs = (P(None, "cols", "rows", None, None), P(None, "rows", None), P(None, "rows", None))
    return jax.shard_map(local, mesh=mesh, in_specs=in_specs, out_specs=out_specs, check_vma=False)
```

```python
import functools

import jax
import jax.numpy as jnp
from jax import lax
from jax.experimental import pallas as pl
from jax.experimental.pallas import tpu as pltpu
from jax.sharding import PartitionSpec as P

BF = jnp.bfloat16
F32 = jnp.float32
ROW_ORDER = (0, 6, 4, 2, 1, 7, 5, 3)
VMEM_BYTES = 32 << 20
FIRST_ORDER = (3, 1, 2)
SUM_ORDER = (3, 2, 1)
LAST_ORDER = (1, 2, 3)


def dot(a, b):
    return jnp.dot(a, b, preferred_element_type=F32)


def dot_nt(a, b):
    return lax.dot_general(a, b, (((1,), (1,)), ((), ())), preferred_element_type=F32)


def pow2(n):
    return n & (n - 1) == 0


def target(i, j, n):
    return i ^ j if pow2(n) else (i + j) % n


def source(i, j, n):
    return i ^ j if pow2(n) else (i - j) % n


def hop(x, axis, j):
    n = lax.axis_size(axis)
    return lax.ppermute(x, axis, [(i, target(i, j, n)) for i in range(n)])


def gather_rows(x):
    n = lax.axis_size("rows")
    me = lax.axis_index("rows")
    if n == 8:
        parts = [x] + [hop(x, "rows", j) for j in (6, 4, 2)]
        offsets = [0, 6, 4, 2]
        here = jnp.stack(parts)
        there = hop(here, "rows", 1)
        whole = jnp.concatenate([here, there], 0)
        offsets = offsets + [o ^ 1 for o in offsets]
        return whole, [source(me, o, n) for o in offsets]
    if pow2(n):
        whole, offsets, bit = x[None], [0], n // 2
        while bit:
            whole = jnp.concatenate([whole, hop(whole, "rows", bit)], 0)
            offsets = offsets + [o ^ bit for o in offsets]
            bit //= 2
        return whole, [source(me, o, n) for o in offsets]
    return lax.all_gather(x, "rows"), list(range(n))


def scatter_cols(pieces):
    n = lax.axis_size("cols")
    me = lax.axis_index("cols")
    total = lax.dynamic_index_in_dim(pieces, me, 0, False).astype(F32)
    for j in reversed(range(1, n)):
        sent = lax.dynamic_index_in_dim(pieces, target(me, j, n), 0, False)
        total = total + hop(sent, "cols", j).astype(F32)
    return total


def gather_cols(x):
    n = lax.axis_size("cols")
    me = lax.axis_index("cols")
    whole = jnp.zeros((n,) + x.shape, x.dtype)
    got = [(me, x)] + [(source(me, j, n), hop(x, "cols", j)) for j in reversed(range(1, n))]
    for at, piece in got:
        whole = lax.dynamic_update_index_in_dim(whole, piece, at, 0)
    return whole


def general(known_inverse, lower_panel, chain_panel, diag_inverse, top_cols, top_diag, pattern):
    n_rows = lax.axis_size("rows")
    n_cols = lax.axis_size("cols")
    row_id = lax.axis_index("rows")
    col_id = lax.axis_index("cols")
    supers = lower_panel.shape[0]
    piece = known_inverse.shape[2]
    width = lower_panel.shape[-1]
    share = width // n_rows
    known = known_inverse.reshape(n_cols * piece, -1)
    group_mask = lax.dynamic_slice_in_dim(pattern, col_id * n_rows, n_rows, 1).astype(BF)
    panels = lower_panel[:, 0] * group_mask[:, :, None, None]
    own_mask = lax.dynamic_index_in_dim(group_mask, row_id, 1, keepdims=False).astype(F32)

    slabs = panels.reshape(supers, n_rows * piece, width)
    partial = jnp.stack([dot(known, slabs[k]).astype(BF).reshape(n_cols, piece, width) for k in range(supers)], 1)
    product = scatter_cols(partial)

    start = [top_diag] + [diag_inverse[k] for k in reversed(range(1, supers))]
    level_of = lambda c: supers - c
    mine = jnp.zeros((share, width), F32)
    for i, s in enumerate(start):
        mine = jnp.where(col_id % len(start) == i, s, mine) if n_cols <= len(start) else jnp.where(col_id == i, s, mine)
    joined = jnp.concatenate([mine.astype(BF), top_cols.reshape(piece, width)], 0)
    gathered, order = gather_rows(joined)
    shares = gathered[:, :share].reshape(width, width)
    tops = gathered[:, share:].reshape(n_rows * piece, width)
    order = jnp.stack([jnp.asarray(o, jnp.int32) for o in order])
    panel_rel = [p[order].reshape(n_rows * piece, width) for p in panels]
    own_rows = (lax.broadcasted_iota(jnp.int32, (share, width), 1) == row_id * share + lax.broadcasted_iota(jnp.int32, (share, width), 0)).astype(BF)
    stacks = [own_rows]
    for k in range(supers):
        stacks.append(jnp.concatenate([dot_nt(stacks[k], chain_panel[k]).astype(BF), own_rows], 0))
    begins = []
    for k in range(supers + 1):
        rel = stacks[k].reshape(-1, n_rows, share)[:, order].reshape(-1, width)
        begins.append(dot(rel, shares))
    reach = [dot_nt(stacks[k], panel_rel[k]).astype(BF) for k in range(supers)]

    prev = top_cols.reshape(piece, width)
    cols_list = [None] * supers
    for k in reversed(range(supers)):
        carried = dot(prev, chain_panel[k])
        prev = (-(product[k] + carried) * own_mask[k]).astype(BF)
        cols_list[k] = prev
    cols_out = jnp.stack(cols_list)
    all_cols, _ = gather_rows(cols_out)
    slab_cols = [all_cols[:, k].reshape(n_rows * piece, width) for k in range(supers)] + [tops]

    acc = jnp.where(col_id == 0, begins[supers], 0.0)
    diag_list = [None] * supers
    sub_list = [None] * supers
    for k in reversed(range(supers)):
        across = dot_nt(stacks[k + 1], slab_cols[k + 1]).astype(BF)
        full = dot(acc.astype(BF), chain_panel[k]) + dot(across, panel_rel[k])
        sub_list[k] = -full[(k + 1) * share:]
        acc = full[: (k + 1) * share] - dot(reach[k], slab_cols[k])
        diag_list[k] = acc[k * share :]
        if k:
            acc = acc + jnp.where(col_id == level_of(k), begins[k], 0.0)
    done = jnp.stack(diag_list + sub_list)
    if share % n_cols == 0:
        part = share // n_cols
        pieces = jnp.swapaxes(done.astype(BF).reshape(2 * supers, n_cols, part, width), 0, 1)
        summed = gather_cols(scatter_cols(pieces).astype(BF))
        summed = jnp.swapaxes(summed, 0, 1).reshape(2 * supers, share, width)
    else:
        summed = lax.psum(done.astype(BF), "cols")
    summed = summed.astype(F32)
    return (
        cols_out.reshape(supers, 1, 1, piece, width),
        diag_inverse + summed[:supers],
        summed[supers:],
    )


def fetch(source, into, sem):
    copy = pltpu.make_async_copy(source, into, sem)
    copy.start()
    return copy


def first_kernel(n_cols, n_rows, g_any, m_any, pattern_any, *refs):
    panel_ref, mask_ref = refs[:2]
    piece_refs = refs[2 : 2 + n_cols]
    g_ref, order_ref, m_ref, pattern_ref, sems = refs[2 + n_cols :]
    col, row = lax.axis_index("cols"), lax.axis_index("rows")
    supers, _, piece, _ = m_ref.shape
    pattern_copy = fetch(pattern_any, pattern_ref, sems.at[0])
    panel_copy = fetch(m_any, m_ref, sems.at[1])
    g_copy = fetch(g_any, g_ref, sems.at[2])
    g_copy.wait()
    for j in range(n_cols):
        order_ref[pl.ds(j * piece, piece)] = g_ref[col ^ j]
    pattern_copy.wait()
    panel_copy.wait()
    for k in range(supers):
        mask_ref[k] = jnp.full(mask_ref.shape[1:], pattern_ref[k, col * n_rows + row].astype(F32))
        for r in range(n_rows):
            on = pattern_ref[k, col * n_rows + r] != 0
            panel_ref[k, pl.ds(r * piece, piece)] = jnp.where(on, m_ref[k, r], jnp.zeros_like(m_ref[k, r]))
        product = dot(order_ref[...], panel_ref[k]).astype(BF)
        for j, out in enumerate(piece_refs):
            out[k] = product[j * piece : (j + 1) * piece]


def chain_kernel(l_ref, carry_ref, mask_ref, own_ref, *refs):
    *got_refs, cols_ref, copy_ref = refs
    supers, piece, _ = own_ref.shape
    carried = carry_ref[...]
    totals = []
    for k in range(supers):
        total = own_ref[k].astype(F32)
        for got in got_refs:
            total = total + got[k].astype(F32)
        totals.append(total)
    for k in reversed(range(supers)):
        total = totals[k] + (carried if k == supers - 1 else dot(prev, l_ref[k]))
        prev = (-(total * mask_ref[k, pl.ds(0, 1)])).astype(BF)
        cols_ref[k] = prev
        copy_ref[k] = prev


def place(refs, order, write):
    me = lax.axis_index("rows")
    for ref, offset in zip(refs, order):
        write(me ^ offset, ref)


def ready_kernel(n_cols, n_rows, l_any, diag_any, top_any, tops_any, panel_ref, *refs):
    l_ref, stacks_ref, reach_ref, joined_ref, carry_ref, begin_ref, tops_ref, sems = refs
    supers, width, _ = l_ref.shape
    share, piece = width // n_rows, tops_ref.shape[0]
    col, row = lax.axis_index("cols"), lax.axis_index("rows")
    copies = [fetch(l_any.at[0], l_ref.at[0], sems.at[0]), fetch(l_any.at[pl.ds(1, supers - 1)], l_ref.at[pl.ds(1, supers - 1)], sems.at[1])]
    tops_copy = fetch(tops_any, tops_ref, sems.at[supers])

    @pl.when(col == 0)
    def _():
        fetch(top_any, begin_ref, sems.at[supers + 1])

    @pl.when(jnp.logical_and(col > 0, col < supers))
    def _():
        fetch(diag_any.at[jnp.clip(supers - col, 1, supers - 1)], begin_ref, sems.at[supers + 1])

    @pl.when(col >= supers)
    def _():
        begin_ref[...] = jnp.zeros_like(begin_ref)

    lane = lax.broadcasted_iota(jnp.int32, (share, width), 1)
    sub = lax.broadcasted_iota(jnp.int32, (share, width), 0)
    unit = jnp.where(lane == row * share + sub, 1.0, 0.0).astype(BF)
    stacks_ref[...] = jnp.zeros_like(stacks_ref)
    stacks_ref[0, pl.ds(0, share)] = unit
    stack, at = unit, 0
    for k in range(supers):
        reach_ref[pl.ds(at, (k + 1) * share)] = dot_nt(stack, panel_ref[k]).astype(BF)
        at += (k + 1) * share
        if k < 2:
            copies[k].wait()
        stack = jnp.concatenate([dot_nt(stack, l_ref[k]).astype(BF), unit], 0)
        stacks_ref[k + 1, pl.ds(0, (k + 2) * share)] = stack
    tops_copy.wait()
    carry_ref[...] = dot(tops_ref[...], l_ref[supers - 1])

    @pl.when(col < supers)
    def _():
        pltpu.make_async_copy(top_any, begin_ref, sems.at[supers + 1]).wait()

    joined_ref[pl.ds(0, share)] = begin_ref[...].astype(BF)
    joined_ref[pl.ds(share, piece)] = tops_ref[...]


def place(refs, order, write):
    me = lax.axis_index("rows")
    for ref, offset in zip(refs, order):
        write(me ^ offset, ref)


def begin_kernel(n_cols, n_rows, order, l_ref, panel_ref, stacks_ref, *refs):
    got = refs[: len(order)]
    begin_ref, ahead_ref, x_ref, y_ref = refs[len(order) :]
    supers, width, _ = l_ref.shape
    share, piece = width // n_rows, y_ref.shape[0] // n_rows
    col = lax.axis_index("cols")

    def write(at, ref):
        x_ref[pl.ds(pl.multiple_of(at * share, share), share)] = ref[pl.ds(0, share)]
        y_ref[pl.ds(pl.multiple_of(at * piece, piece), piece)] = ref[pl.ds(share, piece)]

    place(got, order, write)
    begin = dot(stacks_ref[jnp.maximum(supers - col, 0)], x_ref[...])
    begin_ref[...] = begin
    across = dot_nt(stacks_ref[supers], y_ref[...]).astype(BF)
    ahead_ref[...] = dot(across, panel_ref[supers - 1])

    @pl.when(col == 0)
    def _():
        ahead_ref[...] += dot(begin.astype(BF), l_ref[supers - 1])


def rows_kernel(n_cols, n_rows, order, levels, last, l_ref, panel_ref, stacks_ref, reach_ref, begin_ref, from_ref, *refs):
    got, refs = refs[: len(order)], refs[len(order) :]
    pieces, refs = refs[:n_cols], refs[n_cols:]
    *acc_refs, y_ref, done_ref = refs
    supers, width, _ = l_ref.shape
    share = width // n_rows
    piece = y_ref.shape[1] // n_rows
    part = share // n_cols
    col = lax.axis_index("cols")
    top = levels[0] == supers - 1

    def write(at, ref):
        for k in range(levels[-1], levels[0] + (1 if top else 2)):
            y_ref[k, pl.ds(pl.multiple_of(at * piece, piece), piece)] = ref[k]

    place(got, order, write)
    acc = from_ref[...]
    for i, k in enumerate(levels):
        here = (k + 1) * share
        if k == supers - 1:
            full = acc
        else:
            across = dot_nt(stacks_ref[k + 1, pl.ds(0, here + share)], y_ref[k + 1]).astype(BF)
            full = dot(acc.astype(BF), l_ref[k]) + dot(across, panel_ref[k])
        acc = full[:here] - dot(reach_ref[pl.ds(sum((j + 1) * share for j in range(k)), here)], y_ref[k])
        done_ref[2 * i] = acc[k * share :].astype(BF)
        done_ref[2 * i + 1] = (-full[here:]).astype(BF)
        if k:
            acc = acc + jnp.where(col == supers - k, begin_ref[pl.ds(0, here)], 0.0)
    if not last:
        acc_refs[0][...] = acc
    for j, out in enumerate(pieces):
        out[...] = done_ref[:, pl.ds(pl.multiple_of((col ^ j) * part, part), part)]


def sum_kernel(own_ref, *refs):
    *got_refs, out_ref = refs
    for i in range(own_ref.shape[0]):
        total = own_ref[i].astype(F32)
        for got in got_refs:
            total = total + got[i].astype(F32)
        out_ref[i] = total.astype(BF)


def last_kernel(n_cols, offsets, levels, diag_ref, *refs):
    got_refs = refs[:n_cols]
    diag_out, sub_out, done_ref, sub_ref, sems = refs[-5:]
    part = got_refs[0].shape[1]
    col = lax.axis_index("cols")
    places = [pl.ds(pl.multiple_of((col ^ j) * part, part), part) for j in offsets]
    copies = []
    for i, k in enumerate(levels):
        at = k - levels[-1]
        for rows, got in zip(places, got_refs):
            sub_ref[at, rows] = got[2 * i + 1].astype(F32)
            done_ref[at, rows] = diag_ref[k, rows] + got[2 * i].astype(F32)
        copies.append(fetch(sub_ref.at[at], sub_out.at[k], sems.at[2 * i]))
        copies.append(fetch(done_ref.at[at], diag_out.at[k], sems.at[2 * i + 1]))
    for copy in copies:
        copy.wait()


def call(kernel, outs, *args, scratch=(), away=(), out_away=False, aliases=None, flops=0, moved=0):
    vmem, hbm = pl.BlockSpec(memory_space=pltpu.VMEM), pl.BlockSpec(memory_space=pltpu.HBM)
    return pl.pallas_call(
        kernel,
        out_shape=tuple(jax.ShapeDtypeStruct(s, d) for s, d in outs),
        in_specs=[hbm if i in away else vmem for i in range(len(args))],
        out_specs=tuple(hbm if out_away else vmem for _ in outs),
        input_output_aliases=aliases or {},
        scratch_shapes=scratch,
        compiler_params=pltpu.CompilerParams(vmem_limit_bytes=VMEM_BYTES),
        cost_estimate=pl.CostEstimate(flops=flops, bytes_accessed=moved, transcendentals=0),
    )(*[pltpu.with_memory_space_constraint(a, pltpu.HBM) if i in away else a for i, a in enumerate(args)])


def exchange_rows(x):
    near = [x] + [hop(x, "rows", j) for j in ROW_ORDER[1:4]]
    return near + [hop(p, "rows", 1) for p in near]


def local(known_inverse, lower_panel, chain_panel, diag_inverse, top_cols, top_diag, pattern):
    n_rows = lax.axis_size("rows")
    n_cols = lax.axis_size("cols")
    supers = lower_panel.shape[0]
    piece = known_inverse.shape[2]
    width = lower_panel.shape[-1]
    share = width // n_rows
    if n_rows != len(ROW_ORDER) or n_cols != 1 + len(FIRST_ORDER) or n_cols < supers or share % (16 * n_cols) or piece % 16:
        return general(known_inverse, lower_panel, chain_panel, diag_inverse, top_cols, top_diag, pattern)
    known = known_inverse[:, 0]
    tops = top_cols[0, 0]
    block = n_rows * piece
    ways = range(1, n_cols)
    rows_of = [(k + 1) * share for k in range(supers + 1)]
    panel, mask, own, *sent = call(
        functools.partial(first_kernel, n_cols, n_rows),
        [((supers, block, width), BF), ((supers, 8, width), F32)] + [((supers, piece, width), BF)] * n_cols,
        known, lower_panel[:, 0], pattern, away=range(3),
        scratch=[
            pltpu.VMEM(known.shape, BF), pltpu.VMEM((n_cols * piece, block), BF), pltpu.VMEM((supers, n_rows, piece, width), BF),
            pltpu.SMEM(pattern.shape, jnp.int32), pltpu.SemaphoreType.DMA((3,)),
        ],
        flops=2 * known.size * supers * width, moved=4 * block * width * supers,
    )
    got = [hop(sent[j - 1], "cols", j) for j in FIRST_ORDER]
    links, stacks, reach, joined, carry = call(
        functools.partial(ready_kernel, n_cols, n_rows),
        [(chain_panel.shape, BF), ((supers + 1, rows_of[supers], width), BF), ((sum(rows_of[:supers]), block), BF), ((share + piece, width), BF), ((piece, width), F32)],
        chain_panel, diag_inverse, top_diag, tops, panel, away=range(4),
        scratch=[pltpu.VMEM((share, width), F32), pltpu.VMEM((piece, width), BF), pltpu.SemaphoreType.DMA((supers + 2,))],
        flops=2 * 12 * share * width * width, moved=4 * width * width * supers,
    )
    begin, ahead = call(
        functools.partial(begin_kernel, n_cols, n_rows, ROW_ORDER),
        [((rows_of[supers], width), F32)] * 2,
        links, panel, stacks, *exchange_rows(joined),
        scratch=[pltpu.VMEM((width, width), BF), pltpu.VMEM((block, width), BF)],
        flops=2 * 15 * share * width * width, moved=4 * width * width,
    )
    cols, cols_out = call(
        chain_kernel,
        [((supers, piece, width), BF)] * 2,
        links, carry, mask, own, *got,
        flops=2 * piece * width * width * supers, moved=2 * width * width * supers,
    )
    arrived = exchange_rows(cols)
    split = supers // 2
    groups = [tuple(reversed(range(split, supers))), tuple(reversed(range(split)))]
    state, parts = ahead, []
    for levels in groups:
        last = levels[-1] == 0
        count = 2 * len(levels)
        *pieces, state = call(
            functools.partial(rows_kernel, n_cols, n_rows, ROW_ORDER, levels, last),
            [((count, share // n_cols, width), BF)] * n_cols + ([] if last else [((levels[-1] * share + share, width), F32)]),
            links, panel, stacks, reach, begin, state, *arrived,
            scratch=[pltpu.VMEM((supers, block, width), BF), pltpu.VMEM((count, share, width), BF)],
            flops=2 * 10 * share * width * width, moved=4 * width * width * supers,
        ) + ((None,) if last else ())
        parts.append((levels, pieces))
    sums = []
    for levels, pieces in parts:
        got = [hop(pieces[j], "cols", j) for j in SUM_ORDER]
        sums.append((levels, call(sum_kernel, [(pieces[0].shape, BF)], pieces[0], *got)[0]))
    filled = ()
    for levels, summed in sums:
        offsets = (0,) + LAST_ORDER
        got = [summed] + [hop(summed, "cols", j) for j in offsets[1:]]
        filled = call(
            functools.partial(last_kernel, n_cols, offsets, levels),
            [(diag_inverse.shape, F32)] * 2,
            diag_inverse, *got, *filled, away=range(1 + n_cols, 1 + n_cols + len(filled)), out_away=True,
            aliases={1 + n_cols + i: i for i in range(len(filled))},
            scratch=[pltpu.VMEM((len(levels), share, width), F32)] * 2 + [pltpu.SemaphoreType.DMA((2 * len(levels),))],
        )
    diag, sub = filled
    return cols_out.reshape(supers, 1, 1, piece, width), diag, sub


def solution(mesh):
    in_specs = (
        P(None, "rows", None, "cols"),
        P(None, "cols", None, None, None),
        P(),
        P(None, "rows", None),
        P("cols", "rows", None, None),
        P("rows", None),
        P(),
    )
    out_specs = (P(None, "cols", "rows", None, None), P(None, "rows", None), P(None, "rows", None))
    return jax.shard_map(local, mesh=mesh, in_specs=in_specs, out_specs=out_specs, check_vma=False)
```
